32 devices in a mesh: seq: 16 (over z, y, x), head: 2 (over core).
Axes of the slice: x: 2, y: 2, z: 4, core: 2. Of those that a mesh axis runs over, the one named last changes fastest.
Arguments:
- queries: bfloat16 [8192, 1024], P('seq', 'head'), may hold values from -8 to 8
- keys: bfloat16 [8192, 1024], P('seq', 'head'), may hold values from -8 to 8
- values: bfloat16 [8192, 1024], P('seq', 'head'), may hold values from -6 to 6
- distances: int32 [4], replicated, may hold values from 1 to 8, as said below
- feature_proj: bfloat16 [64, 128], replicated, may hold values from -6 to 6
- out_proj: bfloat16 [1024, 1024], P('head'), may hold values from -0.1875 to 0.1875
Outputs:
- mixed: bfloat16 [8192, 1024], P('seq', 'head')
The draws below stay inside these ranges and needn't reach their ends.
Inputs may be any that keep to these rules, and one draw needn't show every extreme that they name: `distances`: four different powers of two; 1 and 16 // 2 are always among them.
All inputs are finite; a program needn't handle non-finite values.
Results may differ from the reference program's by a relative error of at most 0.018.
Values may be sent and summed in bfloat16 or wider, within the bound.
No kernel may reach another device: no remote copies, remote signals or barrier semaphores. Data moves between devices by JAX's collectives and lax.ppermute only.
A program may use at most 128 MiB of HBM per device.

```python
import jax
import jax.numpy as jnp
from jax import lax

HEADS = 16
HEAD_DIM = 64
FEATURES = 128
PARTNERS = 4
TOK_DEV = 512
SEQ = 8192
N_SEQ = 16


def shared_draw(key, salt):
    width = HEADS * HEAD_DIM
    own_key = jax.random.fold_in(key, salt)
    base = jnp.clip(1.4 * jax.random.normal(own_key, (SEQ, width), jnp.float32), -8.0, 8.0)
    return base.astype(jnp.bfloat16)


def draw_queries(key, part):
    return shared_draw(key, 21)


def draw_keys(key, part):
    return shared_draw(key, 37)


def draw_distances(key, part):
    count = N_SEQ.bit_length() - 1
    middle = jax.random.permutation(jax.random.fold_in(key, 5), count - 2) + 1
    bits = jnp.concatenate([jnp.array([0, count - 1], jnp.int32), middle[:2].astype(jnp.int32)])
    bits = jax.random.permutation(jax.random.fold_in(key, 9), bits)
    return jnp.left_shift(jnp.ones((PARTNERS,), jnp.int32), bits).astype(jnp.int32)


def steps_of(rng, shape, cuts, low, top_value):
    def one(axis_at, shards_of):
        heights = jax.random.uniform(jax.random.fold_in(jax.random.fold_in(rng, 6), axis_at), (shards_of,), jnp.float32, low / len(cuts), top_value / len(cuts))
        return jnp.repeat(jnp.exp(heights), shape[axis_at] // shards_of).reshape((-1,) + (1,) * (len(shape) - axis_at - 1))

    factor_of = one(*cuts[0])
    for cut in cuts[1:]:
        factor_of = factor_of * one(*cut)
    return factor_of


def normal_values(stream_key, shape, spread, most, shards=(), held_as=jnp.bfloat16):
    values = jax.random.normal(stream_key, shape, jnp.float32) * spread
    if len(shards) > 0:
        values = steps_of(stream_key, shape, shards, -0.22, 0.18) * values
    return jnp.clip(values, min=-most, max=most).astype(held_as)


def setup_inputs(seed: int = 0) -> dict:
    streams_of = jax.random.split(jax.random.key(seed), 7)
    queries = draw_queries(jax.random.fold_in(streams_of[6], 71), 0)
    keys = draw_keys(jax.random.fold_in(streams_of[6], 71), 0)
    values = normal_values(streams_of[2], (SEQ, HEADS * HEAD_DIM), 1.0, 6.0, ((0, 16), (1, 2)))
    distances = draw_distances(jax.random.fold_in(streams_of[6], 71), 0)
    feature_proj = normal_values(streams_of[4], (HEAD_DIM, FEATURES), 1.0, 6.0)
    out_proj = normal_values(streams_of[5], (HEADS * HEAD_DIM, HEADS * HEAD_DIM), (HEADS * HEAD_DIM) ** -0.5, 0.1875, ((0, 2),))
    return {"queries": queries, "keys": keys, "values": values, "distances": distances, "feature_proj": feature_proj, "out_proj": out_proj}


def reference(queries, keys, values, distances, feature_proj, out_proj):
    blocks = SEQ // TOK_DEV
    width = HEADS * HEAD_DIM
    q_four = queries.reshape(blocks, TOK_DEV, HEADS, HEAD_DIM)
    k_four = keys.reshape(blocks, TOK_DEV, HEADS, HEAD_DIM)
    v_four = values.reshape(blocks, TOK_DEV, HEADS, HEAD_DIM)
    feat = feature_proj.astype(jnp.float32)
    root_quarter = HEAD_DIM ** -0.25
    root_half = HEAD_DIM ** -0.5

    def key_terms(carry, block):
        k_block, v_block = block
        k_float = k_block.astype(jnp.float32)
        proj = jnp.einsum('thd,dr->thr', k_float, feat)
        square = jnp.sum(k_float * k_float, axis=-1, keepdims=True)
        phi_k = jnp.exp(proj * root_quarter - square * 0.5 * root_half).astype(jnp.bfloat16)
        phi_k = lax.optimization_barrier(phi_k).astype(jnp.float32)
        kv_state = carry[0] + jnp.einsum('thr,the->hre', phi_k, v_block.astype(jnp.float32))
        norm_state = carry[1] + jnp.sum(phi_k, axis=0)
        return (kv_state, norm_state), None

    start = (jnp.zeros((HEADS, FEATURES, HEAD_DIM), jnp.float32), jnp.zeros((HEADS, FEATURES), jnp.float32))
    (kv_state, norm_state), _ = lax.scan(key_terms, start, (k_four, v_four))

    def one_block(index):
        q_float = q_four[index].astype(jnp.float32)
        picks = jnp.concatenate([jnp.reshape(index, (1,)).astype(jnp.int32), jnp.bitwise_xor(index, distances).astype(jnp.int32)])
        k_rows = k_four[picks].reshape(-1, HEADS, HEAD_DIM).astype(jnp.float32)
        v_rows = v_four[picks].reshape(-1, HEADS, HEAD_DIM).astype(jnp.float32)
        scores = jnp.einsum('thd,shd->hts', q_float, k_rows) * root_half
        top = jnp.max(scores, axis=-1, keepdims=True)
        probs = jnp.exp(scores - top)
        weights = lax.optimization_barrier(probs.astype(jnp.bfloat16)).astype(jnp.float32)
        numer = jnp.einsum('hts,shd->htd', weights, v_rows)
        attended = jnp.transpose(numer / jnp.sum(probs, axis=-1)[..., None], (1, 0, 2))
        q_proj = jnp.einsum('thd,dr->thr', q_float, feat) * root_quarter
        phi_q = jnp.exp(q_proj - jnp.max(q_proj, axis=-1, keepdims=True))
        low_numer = jnp.einsum('thr,hre->the', phi_q, kv_state, precision=lax.Precision.HIGHEST)
        low_denom = jnp.einsum('thr,hr->th', phi_q, norm_state, precision=lax.Precision.HIGHEST)
        heads_out = (attended + low_numer / low_denom[..., None]).astype(jnp.bfloat16).reshape(TOK_DEV, width)
        return jnp.dot(heads_out, out_proj, preferred_element_type=jnp.float32).astype(jnp.bfloat16)

    mixed = lax.map(one_block, jnp.arange(blocks, dtype=jnp.int32))
    return mixed.reshape(SEQ, width)
```

```python
import functools

import jax
import jax.numpy as jnp
from jax import lax
from jax.experimental import pallas as pl
from jax.experimental.pallas import tpu as pltpu
from jax.sharding import PartitionSpec as P

HEAD_DIM = 64
PARTNERS = 4
PAIR = 2 * HEAD_DIM
NT = (((1,), (1,)), ((), ()))
VMEM = pl.BlockSpec(memory_space=pltpu.VMEM)
VMEM_LIMIT = 20 * 2**20
COST = pl.CostEstimate(flops=1000, transcendentals=0, bytes_accessed=0)


def low_lanes(rows):
    return lax.broadcasted_iota(jnp.int32, (rows, PAIR), 1) < HEAD_DIM


def half_of(pair, half, other):
    low = low_lanes(pair.shape[0])
    fill = jnp.full_like(pair, other)
    return jnp.where(low, pair, fill) if half == 0 else jnp.where(low, fill, pair)


def cols(ref, c):
    return ref[:, c * PAIR:(c + 1) * PAIR]


def block_of(refs):
    return functools.reduce(jnp.add, [ref[...] for ref in refs])


def weigh_head(q_pair, k_pairs, half):
    q_one = half_of(q_pair, half, 0)
    scores = [lax.dot_general(q_one, k, NT, preferred_element_type=jnp.float32) for k in k_pairs]
    top = functools.reduce(jnp.maximum, [jnp.max(s, axis=-1, keepdims=True) for s in scores])
    return top, [jnp.exp(s - top).astype(jnp.bfloat16) for s in scores]


def scaled(q_pair):
    return q_pair * jnp.asarray(HEAD_DIM ** -0.5, q_pair.dtype)


def add_values(weights, v_pairs, half):
    parts = [
        jnp.dot(w, half_of(v, half, 1), preferred_element_type=jnp.float32)
        for w, v in zip(weights, v_pairs)
    ]
    return functools.reduce(jnp.add, parts)


def numer_denom(first, second):
    low = low_lanes(first.shape[0])
    denom = pltpu.roll(jnp.where(low, second, first), HEAD_DIM, 1)
    return jnp.where(low, first, second), denom


def joined(states):
    top = functools.reduce(jnp.maximum, [t for t, _, _ in states])
    factors = [jnp.exp(t - top) for t, _, _ in states]
    numer = functools.reduce(jnp.add, [n * f for (_, n, _), f in zip(states, factors)])
    denom = functools.reduce(jnp.add, [d * f for (_, _, d), f in zip(states, factors)])
    return top, numer, denom


def kernel_call(body, outs, args, name):
    return pl.pallas_call(
        body,
        out_shape=outs,
        in_specs=[VMEM] * len(args),
        out_specs=jax.tree.map(lambda _: VMEM, outs),
        compiler_params=pltpu.CompilerParams(vmem_limit_bytes=VMEM_LIMIT),
        cost_estimate=COST,
        name=name,
    )(*args)


def pairs_call(body, outs, args, pairs, name):
    def every_pair(*refs):
        for c in range(pairs):
            widths = [ref.shape[1] // pairs for ref in refs]
            body(*[ref.at[:, c * n:(c + 1) * n] for ref, n in zip(refs, widths)])

    outs = [pltpu.VMEM(o.shape, o.dtype) for o in outs]
    return kernel_call(every_pair, outs, args, name)


def attend(q, blocks, before, name):
    tokens, width = q.shape
    args = [q] + [x for block in blocks for x in block] + list(before or [])
    count = 1 + 2 * len(blocks)

    def body(*refs):
        outs = refs[-3:]
        q_pair = scaled(refs[0][...])
        k_pairs = [r[...] for r in refs[1:count:2]]
        v_pairs = [r[...] for r in refs[2:count:2]]
        tops, sums = [], []
        for half in range(2):
            top, weights = weigh_head(q_pair, k_pairs, half)
            tops.append(top)
            sums.append(add_values(weights, v_pairs, half))
        state = (jnp.where(low_lanes(tokens), *tops), *numer_denom(*sums))
        if before is not None:
            state = joined([state, tuple(r[...] for r in refs[count:-3])])
        for out, value in zip(outs, state):
            out[...] = value

    outs = [jax.ShapeDtypeStruct((tokens, width), jnp.float32)] * 3
    return pairs_call(body, outs, args, width // PAIR, name)


def weigh(q, parts, name):
    tokens, width = q.shape
    keys = parts[0].shape[0]

    def body(q_ref, *refs):
        w_out, top_out = refs[-2:]
        q_pair = scaled(q_ref[...])
        k_pair = block_of(refs[:-2])
        tops = []
        for half in range(2):
            top, weights = weigh_head(q_pair, [k_pair], half)
            tops.append(top)
            w_out[:, half * keys:(half + 1) * keys] = weights[0]
        top_out[...] = jnp.where(low_lanes(tokens), *tops)

    outs = [
        jax.ShapeDtypeStruct((tokens, width // HEAD_DIM * keys), jnp.bfloat16),
        jax.ShapeDtypeStruct((tokens, width), jnp.float32),
    ]
    return pairs_call(body, outs, [q] + list(parts), width // PAIR, name)


def gather(before, weights, tops, parts, low_rank, name):
    tokens, width = tops.shape
    keys = parts[0].shape[0]

    def body(*refs):
        w_ref, top_ref, low_ref, out = refs[3], refs[4], refs[-2], refs[-1]
        v_pair = block_of(refs[5:-2])
        sums = [
            add_values([w_ref[:, half * keys:(half + 1) * keys]], [v_pair], half)
            for half in range(2)
        ]
        state = (top_ref[...], *numer_denom(*sums))
        _, numer, denom = joined([tuple(r[...] for r in refs[:3]), state])
        out[...] = (numer / denom + low_ref[...]).astype(jnp.bfloat16)

    args = list(before) + [weights, tops] + list(parts) + [low_rank]
    outs = [jax.ShapeDtypeStruct((tokens, width), jnp.bfloat16)]
    return pairs_call(body, outs, args, width // PAIR, name)[0]


def twice(feat):
    return jnp.concatenate([feat, feat], axis=0)


def state_rows(pairs, features):
    return pairs * features + features


def key_state(k, v, feat):
    tokens, width = k.shape
    pairs, features = width // PAIR, feat.shape[1]
    spread = PAIR // (2 * pairs)

    def body(k_ref, v_ref, feat_ref, out):
        feat_t = twice(feat_ref[...].astype(jnp.float32)).T.astype(jnp.bfloat16)
        lane = lax.broadcasted_iota(jnp.int32, (features, PAIR), 1)
        norms = jnp.zeros((features, PAIR), jnp.float32)
        for c in range(pairs):
            k_pair, v_pair = cols(k_ref, c), cols(v_ref, c)
            k_float = k_pair.astype(jnp.float32)
            square = k_float * k_float
            square_hi = square.astype(jnp.bfloat16)
            square_lo = (square - square_hi.astype(jnp.float32)).astype(jnp.bfloat16)
            parts = []
            for half in range(2):
                proj = lax.dot_general(
                    half_of(feat_t, half, 0), k_pair, NT, preferred_element_type=jnp.float32
                )
                ones = half_of(jnp.ones((16, PAIR), jnp.bfloat16), half, 0)
                size = lax.dot_general(ones, square_hi, NT, preferred_element_type=jnp.float32)
                size += lax.dot_general(ones, square_lo, NT, preferred_element_type=jnp.float32)
                phi = jnp.exp(
                    proj * HEAD_DIM ** -0.25 - size[0:1, :] * (0.5 * HEAD_DIM ** -0.5)
                ).astype(jnp.bfloat16)
                parts.append(
                    jnp.dot(phi, half_of(v_pair, half, 1), preferred_element_type=jnp.float32)
                )
            out[c * features:(c + 1) * features, :] = jnp.where(
                low_lanes(features), parts[0], parts[1]
            ).astype(jnp.bfloat16)
            for half in range(2):
                at = (2 * c + half) * spread
                column = parts[half][:, (1 - half) * HEAD_DIM:(1 - half) * HEAD_DIM + 1]
                norms = jnp.where((lane >= at) & (lane < at + spread), column, norms)
        out[pairs * features:, :] = norms.astype(jnp.bfloat16)

    outs = jax.ShapeDtypeStruct((state_rows(pairs, features), PAIR), jnp.bfloat16)
    return kernel_call(body, outs, [k, v, feat], "key_state")


def low_rank_rows(q, feat, state):
    tokens, width = q.shape
    pairs, features = width // PAIR, feat.shape[1]
    spread = PAIR // (2 * pairs)

    def body(q_ref, feat_ref, state_ref, out):
        feat_two = twice(feat_ref[...])
        norms = state_ref[pairs * features:, :]
        for c in range(pairs):
            q_pair = cols(q_ref, c)
            kv = state_ref[c * features:(c + 1) * features, :]
            low = low_lanes(features)
            parts = []
            for half in range(2):
                proj = jnp.dot(
                    half_of(q_pair, half, 0), feat_two, preferred_element_type=jnp.float32
                ) * HEAD_DIM ** -0.25
                phi = jnp.exp(proj - jnp.max(proj, axis=-1, keepdims=True)).astype(jnp.bfloat16)
                at = (2 * c + half) * spread
                column = jnp.broadcast_to(norms[:, at:at + 1], kv.shape)
                both = jnp.where(low, kv, column) if half == 0 else jnp.where(low, column, kv)
                parts.append(jnp.dot(phi, both, preferred_element_type=jnp.float32))
            numer, denom = numer_denom(*parts)
            out[:, c * PAIR:(c + 1) * PAIR] = numer / denom

    outs = jax.ShapeDtypeStruct((tokens, width), jnp.float32)
    return kernel_call(body, outs, [q, feat, state], "low_rank")


def project(acc, parts, dtype, name):
    tokens, width = parts[0][0].shape[0], parts[0][1].shape[1]

    def body(*refs):
        out = refs[-1]
        rest = list(refs[:-1])
        total = rest.pop(0)[...] if acc is not None else None
        for rows, _, first in parts:
            rows_ref, w_ref = rest.pop(0), rest.pop(0)
            w = w_ref[first:first + rows.shape[1], :]
            part = jnp.dot(rows_ref[...], w, preferred_element_type=jnp.float32)
            total = part if total is None else total + part
        out[...] = total.astype(out.dtype)

    args = ([] if acc is None else [acc]) + [x for rows, w, _ in parts for x in (rows, w)]
    return kernel_call(body, jax.ShapeDtypeStruct((tokens, width), dtype), args, name)


def swapped(shard, axis, distance):
    return lax.ppermute(shard, axis, [(i, i ^ distance) for i in range(lax.axis_size(axis))])


def moved(shard, steps):
    span = lax.axis_size("seq") // 4
    return lax.ppermute(
        shard, "seq", [(a * span + r, b * span + r) for a, b in steps for r in range(span)]
    )


def halves_summed(state, bit, index):
    half = state.shape[0] // 2
    mine = (index >> bit) & 1
    kept = lax.dynamic_slice_in_dim(state, mine * half, half)
    sent = lax.dynamic_slice_in_dim(state, (1 - mine) * half, half)
    return kept + swapped(sent, "seq", 1 << bit)


def halves_joined(half, bit, index):
    far = swapped(half, "seq", 1 << bit)
    mine = (index >> bit) & 1
    return jnp.where(
        mine == 0, jnp.concatenate([half, far], axis=0), jnp.concatenate([far, half], axis=0)
    )


def every_distance(q, k, v, feat, w):
    index = lax.axis_index("seq")
    core = lax.axis_index("head")
    width = q.shape[1]

    first_steps = [(1, 3), (2, 0), (0, 1), (3, 2)]
    second_steps = [(1, 2), (2, 1)]
    edge_steps = [(1, 0), (2, 3)]
    after = lax.optimization_barrier
    k_1 = moved(k, first_steps)
    v_1 = moved(v, first_steps)
    k_near = [swapped(k, "seq", d) for d in (1, 2)]
    sums = attend(q, [(k, v)], None, "attend_own")
    state = key_state(k, v, feat)

    state, k_1, k_near, sums = after((state, k_1, k_near, sums))
    k_2 = moved(k_1, second_steps)
    state = halves_summed(state, 1, index)
    state = halves_summed(state, 0, index)
    state, v_next = after((state, v))
    v_near = [swapped(v_next, "seq", d) for d in (1, 2)]

    state, v_1, k_last = after((state, v_1, k))
    state = state + swapped(state, "seq", 4)
    k_3 = moved(k_last, edge_steps)
    sums = attend(q, [(k_1, v_1)], sums, "attend_first")

    v_near, v_1, v_last, sums = after((v_near, v_1, v, sums))
    v_2 = moved(v_1, second_steps)
    v_3 = moved(v_last, edge_steps)
    state, k_2 = after((state, k_2))
    state = state + swapped(state, "seq", 8)
    sums = attend(q, list(zip(k_near, v_near)), sums, "attend_near")
    state, k_3, sums = after((state, k_3, sums))
    state = halves_joined(state, 0, index)
    state = halves_joined(state, 1, index)

    w_own = lax.dynamic_slice_in_dim(w, core * width, width, axis=1)
    w_far = swapped(lax.dynamic_slice_in_dim(w, (1 - core) * width, width, axis=1), "head", 1)

    last = weigh(q, [k_2, k_3], "weigh_last")
    low = low_rank_rows(q, feat, state)
    rows = gather(sums, *last, [v_2, v_3], low, "gather_last")
    far_rows = swapped(rows, "head", 1)
    acc = project(None, [(rows, w_own, 0)], jnp.float32, "project_own")
    return project(acc, [(far_rows, w_far, 0)], jnp.bfloat16, "project_far")


def chosen_distances(q, k, v, distances, feat, w):
    state = key_state(k, v, feat).astype(jnp.float32)
    state = lax.psum(state, "seq").astype(jnp.bfloat16)
    bits = lax.axis_size("seq").bit_length() - 1
    bit_ids = jnp.arange(bits, dtype=jnp.int32)
    powers = jnp.left_shift(jnp.ones((bits,), jnp.int32), bit_ids)

    def path(bit):
        return lambda pair: (swapped(pair[0], "seq", 1 << bit), swapped(pair[1], "seq", 1 << bit))

    paths = [path(bit) for bit in range(bits)]
    low = low_rank_rows(q, feat, state)
    sums = attend(q, [(k, v)], None, "attend_own")
    for partner in range(PARTNERS):
        picked = jnp.sum(jnp.where(distances[partner] == powers, bit_ids, 0))
        k_far, v_far = lax.switch(picked, paths, (k, v))
        if partner < PARTNERS - 1:
            sums = attend(q, [(k_far, v_far)], sums, "attend_far")
    rows = gather(sums, *weigh(q, [k_far], "weigh_last"), [v_far], low, "gather_last")
    part = jnp.dot(rows, w, preferred_element_type=jnp.float32)
    return lax.psum_scatter(part.astype(jnp.bfloat16), "head", scatter_dimension=1, tiled=True)


def per_device(queries, keys, values, distances, feature_proj, out_proj):
    if lax.axis_size("seq") == 1 << PARTNERS and lax.axis_size("head") == 2:
        return every_distance(queries, keys, values, feature_proj, out_proj)
    return chosen_distances(queries, keys, values, distances, feature_proj, out_proj)


def solution(mesh):
    in_specs = (P("seq", "head"), P("seq", "head"), P("seq", "head"), P(), P(), P("head", None))
    return jax.shard_map(
        per_device, mesh=mesh, in_specs=in_specs, out_specs=P("seq", "head"), check_vma=False
    )
```

```python
import functools

import jax
import jax.numpy as jnp
from jax import lax
from jax.experimental import pallas as pl
from jax.experimental.pallas import tpu as pltpu
from jax.sharding import PartitionSpec as P

HEAD_DIM = 64
PARTNERS = 4
PAIR = 2 * HEAD_DIM
NT = (((1,), (1,)), ((), ()))
VMEM = pl.BlockSpec(memory_space=pltpu.VMEM)
SMEM = pl.BlockSpec(memory_space=pltpu.SMEM)
VMEM_LIMIT = 20 * 2**20
COST = pl.CostEstimate(flops=1000, transcendentals=0, bytes_accessed=0)


def low_lanes(rows):
    return lax.broadcasted_iota(jnp.int32, (rows, PAIR), 1) < HEAD_DIM


def half_of(pair, half, other):
    low = low_lanes(pair.shape[0])
    fill = jnp.full_like(pair, other)
    return jnp.where(low, pair, fill) if half == 0 else jnp.where(low, fill, pair)


def cols(ref, c):
    return ref[:, c * PAIR:(c + 1) * PAIR]


def block_of(refs):
    return functools.reduce(jnp.add, [ref[...] for ref in refs])


def weigh_head(q_pair, k_pairs, half):
    q_one = half_of(q_pair, half, 0)
    scores = [lax.dot_general(q_one, k, NT, preferred_element_type=jnp.float32) for k in k_pairs]
    top = functools.reduce(jnp.maximum, [jnp.max(s, axis=-1, keepdims=True) for s in scores])
    return top, [jnp.exp(s - top).astype(jnp.bfloat16) for s in scores]


def scaled(q_pair):
    return q_pair * jnp.asarray(HEAD_DIM ** -0.5, q_pair.dtype)


def add_values(weights, v_pairs, half):
    parts = [
        jnp.dot(w, half_of(v, half, 1), preferred_element_type=jnp.float32)
        for w, v in zip(weights, v_pairs)
    ]
    return functools.reduce(jnp.add, parts)


def numer_denom(first, second):
    low = low_lanes(first.shape[0])
    denom = pltpu.roll(jnp.where(low, second, first), HEAD_DIM, 1)
    return jnp.where(low, first, second), denom


def joined(states):
    top = functools.reduce(jnp.maximum, [t for t, _, _ in states])
    factors = [jnp.exp(t - top) for t, _, _ in states]
    numer = functools.reduce(jnp.add, [n * f for (_, n, _), f in zip(states, factors)])
    denom = functools.reduce(jnp.add, [d * f for (_, _, d), f in zip(states, factors)])
    return top, numer, denom


def kernel_call(body, outs, args, name):
    return pl.pallas_call(
        body,
        out_shape=[pltpu.VMEM(o.shape, o.dtype) for o in outs],
        in_specs=[SMEM if a.dtype == jnp.int32 else VMEM for a in args],
        out_specs=[VMEM] * len(outs),
        compiler_params=pltpu.CompilerParams(vmem_limit_bytes=VMEM_LIMIT),
        cost_estimate=COST,
        name=name,
    )(*args)


def whole(array):
    return [(array, 0, array.shape[1])]


def pairs_call(body, outs, operands, pairs, total, name):
    arrays, places = [], {}
    for c in pairs:
        for number, operand in enumerate(operands):
            share = sum(count for _, _, count in operand) // total
            at = c * share
            for array, first, count in operand:
                if 0 <= at < count:
                    if not any(array is other for other in arrays):
                        arrays.append(array)
                    index = [array is other for other in arrays].index(True)
                    places[c, number] = index, slice(first + at, first + at + share)
                at -= count

    def every_pair(*refs):
        for c in pairs:
            spots = [places[c, number] for number in range(len(operands))]
            ins = [refs[index].at[:, part] for index, part in spots]
            results = []
            for ref in refs[len(arrays):]:
                share = ref.shape[1] // len(pairs)
                at = (c - pairs.start) * share
                results.append(ref.at[:, at:at + share])
            body(*ins, *results)

    return kernel_call(every_pair, outs, arrays, name)


def attend(q, blocks, before, name):
    tokens, width = q.shape
    operands = [whole(q)] + [x for block in blocks for x in block]
    count = len(operands)
    operands += [whole(x) for x in before or []]

    def body(*refs):
        outs = refs[-3:]
        q_pair = scaled(refs[0][...])
        k_pairs = [r[...] for r in refs[1:count:2]]
        v_pairs = [r[...] for r in refs[2:count:2]]
        tops, sums = [], []
        for half in range(2):
            top, weights = weigh_head(q_pair, k_pairs, half)
            tops.append(top)
            sums.append(add_values(weights, v_pairs, half))
        state = (jnp.where(low_lanes(tokens), *tops), *numer_denom(*sums))
        if before is not None:
            state = joined([state, tuple(r[...] for r in refs[count:-3])])
        for out, value in zip(outs, state):
            out[...] = value

    outs = [jax.ShapeDtypeStruct((tokens, width), jnp.float32)] * 3
    return pairs_call(body, outs, operands, range(width // PAIR), width // PAIR, name)


def weigh(q, parts, name):
    tokens, width = q.shape
    keys = parts[0][0][0].shape[0]

    def body(q_ref, *refs):
        w_out, top_out = refs[-2:]
        q_pair = scaled(q_ref[...])
        k_pair = block_of(refs[:-2])
        tops = []
        for half in range(2):
            top, weights = weigh_head(q_pair, [k_pair], half)
            tops.append(top)
            w_out[:, half * keys:(half + 1) * keys] = weights[0]
        top_out[...] = jnp.where(low_lanes(tokens), *tops)

    outs = [
        jax.ShapeDtypeStruct((tokens, width // HEAD_DIM * keys), jnp.bfloat16),
        jax.ShapeDtypeStruct((tokens, width), jnp.float32),
    ]
    return pairs_call(body, outs, [whole(q)] + list(parts), range(width // PAIR), width // PAIR, name)


def gather(before, weights, tops, parts, low_rank, pairs, name):
    tokens = tops.shape[0]
    keys = weights.shape[1] // (tops.shape[1] // HEAD_DIM)

    def body(*refs):
        w_ref, low_ref, out = refs[3], refs[-2], refs[-1]
        v_pair = block_of(refs[5:-2])
        sums = [
            add_values([w_ref[:, half * keys:(half + 1) * keys]], [v_pair], half)
            for half in range(2)
        ]
        state = (refs[4][...], *numer_denom(*sums))
        _, numer, denom = joined([tuple(r[...] for r in refs[:3]), state])
        out[...] = (numer / denom + low_ref[...]).astype(jnp.bfloat16)

    operands = [whole(x) for x in before] + [whole(weights), whole(tops)] + list(parts) + [whole(low_rank)]
    outs = [jax.ShapeDtypeStruct((tokens, len(pairs) * PAIR), jnp.bfloat16)]
    return pairs_call(body, outs, operands, pairs, tops.shape[1] // PAIR, name)[0]


def twice(feat):
    return jnp.concatenate([feat, feat], axis=0)


def state_rows(pairs, features):
    return pairs * features + features


def key_state(k, v, feat):
    tokens, width = k.shape
    pairs, features = width // PAIR, feat.shape[1]
    spread = PAIR // (2 * pairs)

    def body(k_ref, v_ref, feat_ref, out):
        feat_t = twice(feat_ref[...].astype(jnp.float32)).T.astype(jnp.bfloat16)
        lane = lax.broadcasted_iota(jnp.int32, (features, PAIR), 1)
        norms = jnp.zeros((features, PAIR), jnp.float32)
        for c in range(pairs):
            k_pair, v_pair = cols(k_ref, c), cols(v_ref, c)
            k_float = k_pair.astype(jnp.float32)
            square = k_float * k_float
            square_hi = square.astype(jnp.bfloat16)
            square_lo = (square - square_hi.astype(jnp.float32)).astype(jnp.bfloat16)
            parts = []
            for half in range(2):
                proj = lax.dot_general(
                    half_of(feat_t, half, 0), k_pair, NT, preferred_element_type=jnp.float32
                )
                ones = half_of(jnp.ones((16, PAIR), jnp.bfloat16), half, 0)
                size = lax.dot_general(ones, square_hi, NT, preferred_element_type=jnp.float32)
                size += lax.dot_general(ones, square_lo, NT, preferred_element_type=jnp.float32)
                phi = jnp.exp(
                    proj * HEAD_DIM ** -0.25 - size[0:1, :] * (0.5 * HEAD_DIM ** -0.5)
                ).astype(jnp.bfloat16)
                parts.append(
                    jnp.dot(phi, half_of(v_pair, half, 1), preferred_element_type=jnp.float32)
                )
            out[c * features:(c + 1) * features, :] = jnp.where(
                low_lanes(features), parts[0], parts[1]
            ).astype(jnp.bfloat16)
            for half in range(2):
                at = (2 * c + half) * spread
                column = parts[half][:, (1 - half) * HEAD_DIM:(1 - half) * HEAD_DIM + 1]
                norms = jnp.where((lane >= at) & (lane < at + spread), column, norms)
        out[pairs * features:, :] = norms.astype(jnp.bfloat16)

    outs = jax.ShapeDtypeStruct((state_rows(pairs, features), PAIR), jnp.bfloat16)
    return kernel_call(body, [outs], [k, v, feat], "key_state")[0]


def low_rank_rows(q, feat, state):
    tokens, width = q.shape
    pairs, features = width // PAIR, feat.shape[1]
    spread = PAIR // (2 * pairs)

    def body(q_ref, feat_ref, state_ref, out):
        feat_two = twice(feat_ref[...])
        norms = state_ref[pairs * features:, :]
        for c in range(pairs):
            q_pair = cols(q_ref, c)
            kv = state_ref[c * features:(c + 1) * features, :]
            low = low_lanes(features)
            parts = []
            for half in range(2):
                proj = jnp.dot(
                    half_of(q_pair, half, 0), feat_two, preferred_element_type=jnp.float32
                ) * HEAD_DIM ** -0.25
                phi = jnp.exp(proj - jnp.max(proj, axis=-1, keepdims=True)).astype(jnp.bfloat16)
                at = (2 * c + half) * spread
                column = jnp.broadcast_to(norms[:, at:at + 1], kv.shape)
                both = jnp.where(low, kv, column) if half == 0 else jnp.where(low, column, kv)
                parts.append(jnp.dot(phi, both, preferred_element_type=jnp.float32))
            numer, denom = numer_denom(*parts)
            out[:, c * PAIR:(c + 1) * PAIR] = numer / denom

    outs = jax.ShapeDtypeStruct((tokens, width), jnp.float32)
    return kernel_call(body, [outs], [q, feat, state], "low_rank")[0]


def project(acc, parts, name):
    tokens, width = parts[0][0].shape[0], parts[0][1].shape[1]
    arrays = []
    for array in [x for rows, w, _ in parts for x in (rows, w)] + ([] if acc is None else [acc]):
        if not any(array is other for other in arrays):
            arrays.append(array)

    def body(*refs):
        def ref_of(array):
            return refs[[array is other for other in arrays].index(True)]

        total = None if acc is None else ref_of(acc)[...]
        for rows, w, first in parts:
            w_rows = ref_of(w)[first:first + rows.shape[1], :]
            part = jnp.dot(ref_of(rows)[...], w_rows, preferred_element_type=jnp.float32)
            total = part if total is None else total + part
        refs[-1][...] = total.astype(refs[-1].dtype)

    if acc is None:
        outs = [jax.ShapeDtypeStruct((tokens, width), jnp.float32)]
        return kernel_call(body, outs, arrays, name)[0]
    return pl.pallas_call(
        body,
        out_shape=jax.ShapeDtypeStruct((tokens, width), jnp.bfloat16),
        in_specs=[VMEM] * len(arrays),
        out_specs=VMEM,
        compiler_params=pltpu.CompilerParams(vmem_limit_bytes=VMEM_LIMIT),
        cost_estimate=COST,
        name=name,
    )(*arrays)


def parted(array, place, bit, axis, name):
    shape = list(array.shape)
    shape[axis] //= 2
    half = shape[axis]

    def body(place_ref, ref, kept, sent):
        mine = (place_ref[0] >> bit) & 1
        for out, at in ((kept, mine), (sent, 1 - mine)):
            rows = pl.ds(pl.multiple_of(at * half, half), half)
            out[...] = ref[rows, :] if axis == 0 else ref[:, rows]

    outs = [jax.ShapeDtypeStruct(tuple(shape), array.dtype)] * 2
    return kernel_call(body, outs, [place, array], name)


def packed(k, v, split, name):
    tokens, width = k.shape

    def body(k_ref, v_ref, x_out, y_out, done):
        copies = [
            pltpu.make_async_copy(k_ref, x_out.at[:, pl.ds(0, width)], done.at[0]),
            pltpu.make_async_copy(
                v_ref.at[:, pl.ds(0, split)], x_out.at[:, pl.ds(width, split)], done.at[1]
            ),
            pltpu.make_async_copy(v_ref.at[:, pl.ds(split, width - split)], y_out, done.at[2]),
        ]
        for copy in copies:
            copy.start()
        for copy in copies:
            copy.wait()

    return pl.pallas_call(
        body,
        out_shape=[
            pltpu.VMEM((tokens, width + split), k.dtype),
            pltpu.VMEM((tokens, width - split), k.dtype),
        ],
        in_specs=[pl.BlockSpec(memory_space=pl.ANY)] * 2,
        out_specs=[VMEM] * 2,
        scratch_shapes=[pltpu.SemaphoreType.DMA((3,))],
        cost_estimate=COST,
        name=name,
    )(k, v)


def added(first, second, name):
    def body(first_ref, second_ref, out):
        out[...] = first_ref[...] + second_ref[...]

    return kernel_call(body, [jax.ShapeDtypeStruct(first.shape, first.dtype)], [first, second], name)[0]


def added_parted(first, second, place, bit, name):
    half = first.shape[0] // 2

    def body(place_ref, first_ref, second_ref, kept, sent):
        mine = (place_ref[0] >> bit) & 1
        for out, at in ((kept, mine), (sent, 1 - mine)):
            rows = pl.ds(pl.multiple_of(at * half, half), half)
            out[...] = first_ref[rows, :] + second_ref[rows, :]

    outs = [jax.ShapeDtypeStruct((half, first.shape[1]), first.dtype)] * 2
    return kernel_call(body, outs, [place, first, second], name)


def placed(own, far, place, bit, name):
    half = own.shape[0]

    def body(place_ref, own_ref, far_ref, out):
        mine = (place_ref[0] >> bit) & 1
        for ref, at in ((own_ref, mine), (far_ref, 1 - mine)):
            out[pl.ds(pl.multiple_of(at * half, half), half), :] = ref[...]

    outs = [jax.ShapeDtypeStruct((2 * half, own.shape[1]), own.dtype)]
    return kernel_call(body, outs, [place, own, far], name)[0]


def swapped(shard, axis, distance):
    return lax.ppermute(shard, axis, [(i, i ^ distance) for i in range(lax.axis_size(axis))])


def moved(shard, steps):
    span = lax.axis_size("seq") // 4
    return lax.ppermute(
        shard, "seq", [(a * span + r, b * span + r) for a, b in steps for r in range(span)]
    )


def every_distance(q, k, v, feat, w):
    index = lax.axis_index("seq").astype(jnp.int32).reshape(1)
    core = lax.axis_index("head").astype(jnp.int32).reshape(1)
    width = q.shape[1]

    first_steps = [(1, 3), (2, 0), (0, 1), (3, 2)]
    second_steps = [(1, 2), (2, 1)]
    edge_steps = [(1, 0), (2, 3)]
    after = lax.optimization_barrier
    pairs = width // PAIR
    split = pairs // 2 * PAIR

    def k_of(x):
        return [(x, 0, width)]

    def v_of(x, y):
        return [(x, width, split), (y, 0, width - split)]

    k, index, core = after((k, index, core))
    x_own, y_own = packed(k, v, split, "values_packed")
    x_1 = moved(x_own, first_steps)
    k_near = [swapped(k, "seq", d) for d in (1, 2)]
    sums = attend(q, [(whole(k), whole(v))], None, "attend_own")
    state = key_state(k, v, feat)

    state, k_near, sums = after((state, k_near, sums))
    kept, sent = parted(state, index, 1, 0, "state_parted")
    kept, sent = added_parted(kept, swapped(sent, "seq", 2), index, 0, "state_second")
    state = added(kept, swapped(sent, "seq", 1), "state_third")

    state, v_next, y_own = after((state, v, y_own))
    v_near = [swapped(v_next, "seq", d) for d in (1, 2)]
    y_1 = moved(y_own, first_steps)
    state = added(state, swapped(state, "seq", 4), "state_fourth")
    state, x_1 = after((state, x_1))
    far_state = swapped(state, "seq", 8)
    x_2 = moved(x_1, second_steps)

    y_1, far_state, x_own, y_own = after((y_1, far_state, x_own, y_own))
    x_3 = moved(x_own, edge_steps)
    sums = attend(q, [(k_of(x_1), v_of(x_1, y_1))], sums, "attend_first")
    state = added(state, far_state, "state_summed")

    v_near, y_1, y_own, sums, w, state = after((v_near, y_1, y_own, sums, w, state))
    w_own, w_sent = parted(w, core, 0, 1, "weights_parted")
    w_far = swapped(w_sent, "head", 1)
    y_2 = moved(y_1, second_steps)
    y_3 = moved(y_own, edge_steps)
    state = placed(state, swapped(state, "seq", 1), index, 0, "state_joined")
    near = [(whole(k_far), whole(v_far)) for k_far, v_far in zip(k_near, v_near)]
    sums = attend(q, near, sums, "attend_near")
    state, sums, w_far = after((state, sums, w_far))
    state = placed(state, swapped(state, "seq", 2), index, 1, "state_whole")

    low = low_rank_rows(q, feat, state)
    last = weigh(q, [k_of(x_2), k_of(x_3)], "weigh_last")
    v_last = [v_of(x_2, y_2), v_of(x_3, y_3)]
    rows_a = gather(sums, *last, v_last, low, range(0, pairs // 2), "gather_a")
    far_a = swapped(rows_a, "head", 1)
    rows_b = gather(sums, *last, v_last, low, range(pairs // 2, pairs), "gather_b")
    far_b = swapped(rows_b, "head", 1)
    acc = project(None, [(rows_a, w_own, 0), (far_a, w_far, 0), (rows_b, w_own, split)], "project_a")
    return project(acc, [(far_b, w_far, split)], "project_b")


def chosen_distances(q, k, v, distances, feat, w):
    state = key_state(k, v, feat).astype(jnp.float32)
    state = lax.psum(state, "seq").astype(jnp.bfloat16)
    bits = lax.axis_size("seq").bit_length() - 1
    bit_ids = jnp.arange(bits, dtype=jnp.int32)
    powers = jnp.left_shift(jnp.ones((bits,), jnp.int32), bit_ids)

    def path(bit):
        return lambda pair: (swapped(pair[0], "seq", 1 << bit), swapped(pair[1], "seq", 1 << bit))

    paths = [path(bit) for bit in range(bits)]
    low = low_rank_rows(q, feat, state)
    sums = attend(q, [(whole(k), whole(v))], None, "attend_own")
    for partner in range(PARTNERS):
        picked = jnp.sum(jnp.where(distances[partner] == powers, bit_ids, 0))
        k_far, v_far = lax.switch(picked, paths, (k, v))
        if partner < PARTNERS - 1:
            sums = attend(q, [(whole(k_far), whole(v_far))], sums, "attend_far")
    last = weigh(q, [whole(k_far)], "weigh_last")
    pairs = range(q.shape[1] // PAIR)
    rows = gather(sums, *last, [whole(v_far)], low, pairs, "gather_last")
    part = jnp.dot(rows, w, preferred_element_type=jnp.float32)
    return lax.psum_scatter(part.astype(jnp.bfloat16), "head", scatter_dimension=1, tiled=True)


def per_device(queries, keys, values, distances, feature_proj, out_proj):
    if lax.axis_size("seq") == 1 << PARTNERS and lax.axis_size("head") == 2:
        return every_distance(queries, keys, values, feature_proj, out_proj)
    return chosen_distances(queries, keys, values, distances, feature_proj, out_proj)


def solution(mesh):
    in_specs = (P("seq", "head"), P("seq", "head"), P("seq", "head"), P(), P(), P("head", None))
    return jax.shard_map(
        per_device, mesh=mesh, in_specs=in_specs, out_specs=P("seq", "head"), check_vma=False
    )
```

```python
import functools

import jax
import jax.numpy as jnp
from jax import lax
from jax.experimental import pallas as pl
from jax.experimental.pallas import tpu as pltpu
from jax.sharding import PartitionSpec as P

HEAD_DIM = 64
PARTNERS = 4
PAIR = 2 * HEAD_DIM
NT = (((1,), (1,)), ((), ()))
VMEM = pl.BlockSpec(memory_space=pltpu.VMEM)
SMEM = pl.BlockSpec(memory_space=pltpu.SMEM)
VMEM_LIMIT = 20 * 2**20
COST = pl.CostEstimate(flops=1000, transcendentals=0, bytes_accessed=0)


def low_lanes(rows):
    return lax.broadcasted_iota(jnp.int32, (rows, PAIR), 1) < HEAD_DIM


def half_of(pair, half, other):
    low = low_lanes(pair.shape[0])
    fill = jnp.full_like(pair, other)
    return jnp.where(low, pair, fill) if half == 0 else jnp.where(low, fill, pair)


def cols(ref, c):
    return ref[:, c * PAIR:(c + 1) * PAIR]


def block_of(refs):
    return functools.reduce(jnp.add, [ref[...] for ref in refs])


def weigh_head(q_pair, k_pairs, half):
    q_one = half_of(q_pair, half, 0)
    scores = [lax.dot_general(q_one, k, NT, preferred_element_type=jnp.float32) for k in k_pairs]
    top = functools.reduce(jnp.maximum, [jnp.max(s, axis=-1, keepdims=True) for s in scores])
    return top, [jnp.exp(s - top).astype(jnp.bfloat16) for s in scores]


def scaled(q_pair):
    return q_pair * jnp.asarray(HEAD_DIM ** -0.5, q_pair.dtype)


def add_values(weights, v_pairs, half):
    parts = [
        jnp.dot(w, half_of(v, half, 1), preferred_element_type=jnp.float32)
        for w, v in zip(weights, v_pairs)
    ]
    return functools.reduce(jnp.add, parts)


def numer_denom(first, second):
    low = low_lanes(first.shape[0])
    denom = pltpu.roll(jnp.where(low, second, first), HEAD_DIM, 1)
    return jnp.where(low, first, second), denom


def joined(states):
    top = functools.reduce(jnp.maximum, [t for t, _, _ in states])
    factors = [jnp.exp(t - top) for t, _, _ in states]
    numer = functools.reduce(jnp.add, [n * f for (_, n, _), f in zip(states, factors)])
    denom = functools.reduce(jnp.add, [d * f for (_, _, d), f in zip(states, factors)])
    return top, numer, denom


def kernel_call(body, outs, args, name):
    return pl.pallas_call(
        body,
        out_shape=[pltpu.VMEM(o.shape, o.dtype) for o in outs],
        in_specs=[SMEM if a.dtype == jnp.int32 else VMEM for a in args],
        out_specs=[VMEM] * len(outs),
        compiler_params=pltpu.CompilerParams(vmem_limit_bytes=VMEM_LIMIT),
        cost_estimate=COST,
        name=name,
    )(*args)


def whole(array):
    return [(array, 0, array.shape[1])]


def pairs_call(body, outs, operands, pairs, total, name):
    arrays, places = [], {}
    for c in pairs:
        for number, operand in enumerate(operands):
            share = sum(count for _, _, count in operand) // total
            at = c * share
            for array, first, count in operand:
                if 0 <= at < count:
                    if not any(array is other for other in arrays):
                        arrays.append(array)
                    index = [array is other for other in arrays].index(True)
                    places[c, number] = index, slice(first + at, first + at + share)
                at -= count

    def every_pair(*refs):
        for c in pairs:
            spots = [places[c, number] for number in range(len(operands))]
            ins = [refs[index].at[:, part] for index, part in spots]
            results = []
            for ref in refs[len(arrays):]:
                share = ref.shape[1] // len(pairs)
                at = (c - pairs.start) * share
                results.append(ref.at[:, at:at + share])
            body(*ins, *results)

    return kernel_call(every_pair, outs, arrays, name)


def attend(q, blocks, before, name):
    tokens, width = q.shape
    operands = [whole(q)] + [x for block in blocks for x in block]
    count = len(operands)
    operands += [whole(x) for x in before or []]

    def body(*refs):
        outs = refs[-3:]
        q_pair = scaled(refs[0][...])
        k_pairs = [r[...] for r in refs[1:count:2]]
        v_pairs = [r[...] for r in refs[2:count:2]]
        tops, sums = [], []
        for half in range(2):
            top, weights = weigh_head(q_pair, k_pairs, half)
            tops.append(top)
            sums.append(add_values(weights, v_pairs, half))
        state = (jnp.where(low_lanes(tokens), *tops), *numer_denom(*sums))
        if before is not None:
            state = joined([state, tuple(r[...] for r in refs[count:-3])])
        for out, value in zip(outs, state):
            out[...] = value

    outs = [jax.ShapeDtypeStruct((tokens, width), jnp.float32)] * 3
    return pairs_call(body, outs, operands, range(width // PAIR), width // PAIR, name)


def weigh(q, blocks, name):
    tokens, width = q.shape
    keys = blocks[0][0][0][0].shape[0]
    count = len(blocks)

    def body(q_ref, *refs):
        w_out, top_out = refs[-2:]
        q_pair = scaled(q_ref[...])
        rest = list(refs[:-2])
        k_pairs = [block_of([rest.pop(0) for _ in block]) for block in blocks]
        tops = []
        for half in range(2):
            top, weights = weigh_head(q_pair, k_pairs, half)
            tops.append(top)
            for i, w in enumerate(weights):
                at = (half * count + i) * keys
                w_out[:, at:at + keys] = w
        top_out[...] = jnp.where(low_lanes(tokens), *tops)

    outs = [
        jax.ShapeDtypeStruct((tokens, width // HEAD_DIM * count * keys), jnp.bfloat16),
        jax.ShapeDtypeStruct((tokens, width), jnp.float32),
    ]
    operands = [whole(q)] + [part for block in blocks for part in block]
    return pairs_call(body, outs, operands, range(width // PAIR), width // PAIR, name)


def gather(before, weighed, blocks, low_rank, pairs, name):
    weights, tops = weighed
    tokens, width = tops.shape
    count = len(blocks)
    keys = weights.shape[1] // (width // HEAD_DIM) // count
    operands = [whole(x) for x in (*before, weights, tops)]
    operands += [part for block in blocks for part in block]
    if low_rank is not None:
        operands.append(whole(low_rank))

    def body(*refs):
        rest = list(refs[5:len(operands)])
        v_pairs = [block_of([rest.pop(0) for _ in block]) for block in blocks]
        sums = []
        for half in range(2):
            ats = [(half * count + i) * keys for i in range(count)]
            sums.append(add_values([refs[3][:, at:at + keys] for at in ats], v_pairs, half))
        state = joined([tuple(r[...] for r in refs[:3]), (refs[4][...], *numer_denom(*sums))])
        if low_rank is not None:
            state = [(state[1] / state[2] + rest[0][...]).astype(jnp.bfloat16)]
        for out, value in zip(refs[len(operands):], state):
            out[...] = value

    if low_rank is not None:
        outs = [jax.ShapeDtypeStruct((tokens, len(pairs) * PAIR), jnp.bfloat16)]
        return pairs_call(body, outs, operands, pairs, width // PAIR, name)[0]
    outs = [jax.ShapeDtypeStruct((tokens, width), jnp.float32)] * 3
    return pairs_call(body, outs, operands, pairs, width // PAIR, name)


def finish(q, parts, before, low_rank, pairs, name):
    tokens, width = q.shape
    count = len(parts)
    operands = [whole(q)] + [k for k, _ in parts] + [v for _, v in parts]
    operands += [whole(x) for x in (*before, low_rank)]

    def body(*refs):
        q_pair = scaled(refs[0][...])
        k_pair, v_pair = block_of(refs[1:1 + count]), block_of(refs[1 + count:1 + 2 * count])
        tops, sums = [], []
        for half in range(2):
            top, weights = weigh_head(q_pair, [k_pair], half)
            tops.append(top)
            sums.append(add_values(weights, [v_pair], half))
        state = (jnp.where(low_lanes(tokens), *tops), *numer_denom(*sums))
        _, numer, denom = joined([state, tuple(r[...] for r in refs[1 + 2 * count:-2])])
        refs[-1][...] = (numer / denom + refs[-2][...]).astype(jnp.bfloat16)

    outs = [jax.ShapeDtypeStruct((tokens, len(pairs) * PAIR), jnp.bfloat16)]
    return pairs_call(body, outs, operands, pairs, width // PAIR, name)[0]


def twice(feat):
    return jnp.concatenate([feat, feat], axis=0)


def state_rows(pairs, features):
    return pairs * features + features


def key_state(k, v, feat, pairs):
    features = feat.shape[1]
    spread = PAIR // (2 * pairs)
    arrays = []
    for array, _, _ in k + v:
        if not any(array is other for other in arrays):
            arrays.append(array)

    def pair_of(refs, operand, c):
        at = c * PAIR
        for array, first, count in operand:
            if 0 <= at < count:
                index = [array is other for other in arrays].index(True)
                return refs[index][:, first + at:first + at + PAIR]
            at -= count

    def body(*refs):
        feat_ref, out = refs[-2:]
        feat_t = twice(feat_ref[...].astype(jnp.float32)).T.astype(jnp.bfloat16)
        lane = lax.broadcasted_iota(jnp.int32, (features, PAIR), 1)
        norms = jnp.zeros((features, PAIR), jnp.float32)
        for c in range(pairs):
            k_pair, v_pair = pair_of(refs, k, c), pair_of(refs, v, c)
            k_float = k_pair.astype(jnp.float32)
            square = k_float * k_float
            square_hi = square.astype(jnp.bfloat16)
            square_lo = (square - square_hi.astype(jnp.float32)).astype(jnp.bfloat16)
            parts = []
            for half in range(2):
                proj = lax.dot_general(
                    half_of(feat_t, half, 0), k_pair, NT, preferred_element_type=jnp.float32
                )
                ones = half_of(jnp.ones((16, PAIR), jnp.bfloat16), half, 0)
                size = lax.dot_general(ones, square_hi, NT, preferred_element_type=jnp.float32)
                size += lax.dot_general(ones, square_lo, NT, preferred_element_type=jnp.float32)
                phi = jnp.exp(
                    proj * HEAD_DIM ** -0.25 - size[0:1, :] * (0.5 * HEAD_DIM ** -0.5)
                ).astype(jnp.bfloat16)
                parts.append(
                    jnp.dot(phi, half_of(v_pair, half, 1), preferred_element_type=jnp.float32)
                )
            out[c * features:(c + 1) * features, :] = jnp.where(
                low_lanes(features), parts[0], parts[1]
            ).astype(jnp.bfloat16)
            for half in range(2):
                at = (2 * c + half) * spread
                column = parts[half][:, (1 - half) * HEAD_DIM:(1 - half) * HEAD_DIM + 1]
                norms = jnp.where((lane >= at) & (lane < at + spread), column, norms)
        out[pairs * features:, :] = norms.astype(jnp.bfloat16)

    outs = jax.ShapeDtypeStruct((state_rows(pairs, features), PAIR), jnp.bfloat16)
    return kernel_call(body, [outs], arrays + [feat], "key_state")[0]


def low_rank_rows(q, feat, state):
    tokens, width = q.shape
    pairs, features = width // PAIR, feat.shape[1]
    spread = PAIR // (2 * pairs)

    def body(q_ref, feat_ref, state_ref, out):
        feat_two = twice(feat_ref[...])
        norms = state_ref[pairs * features:, :]
        for c in range(pairs):
            q_pair = cols(q_ref, c)
            kv = state_ref[c * features:(c + 1) * features, :]
            low = low_lanes(features)
            parts = []
            for half in range(2):
                proj = jnp.dot(
                    half_of(q_pair, half, 0), feat_two, preferred_element_type=jnp.float32
                ) * HEAD_DIM ** -0.25
                phi = jnp.exp(proj - jnp.max(proj, axis=-1, keepdims=True)).astype(jnp.bfloat16)
                at = (2 * c + half) * spread
                column = jnp.broadcast_to(norms[:, at:at + 1], kv.shape)
                both = jnp.where(low, kv, column) if half == 0 else jnp.where(low, column, kv)
                parts.append(jnp.dot(phi, both, preferred_element_type=jnp.float32))
            numer, denom = numer_denom(*parts)
            out[:, c * PAIR:(c + 1) * PAIR] = numer / denom

    outs = jax.ShapeDtypeStruct((tokens, width), jnp.float32)
    return kernel_call(body, [outs], [q, feat, state], "low_rank")[0]


def project(acc, parts, name):
    tokens, width = parts[0][0].shape[0], parts[0][1].shape[1]
    arrays = []
    for array in [x for rows, w, _ in parts for x in (rows, w)] + ([] if acc is None else [acc]):
        if not any(array is other for other in arrays):
            arrays.append(array)

    def body(*refs):
        def ref_of(array):
            return refs[[array is other for other in arrays].index(True)]

        total = None if acc is None else ref_of(acc)[...]
        for rows, w, first in parts:
            w_rows = ref_of(w)[first:first + rows.shape[1], :]
            part = jnp.dot(ref_of(rows)[...], w_rows, preferred_element_type=jnp.float32)
            total = part if total is None else total + part
        refs[-1][...] = total.astype(refs[-1].dtype)

    if acc is None:
        outs = [jax.ShapeDtypeStruct((tokens, width), jnp.float32)]
        return kernel_call(body, outs, arrays, name)[0]
    return pl.pallas_call(
        body,
        out_shape=jax.ShapeDtypeStruct((tokens, width), jnp.bfloat16),
        in_specs=[VMEM] * len(arrays),
        out_specs=VMEM,
        compiler_params=pltpu.CompilerParams(vmem_limit_bytes=VMEM_LIMIT),
        cost_estimate=COST,
        name=name,
    )(*arrays)


def parted(array, place, bit, axis, name):
    shape = list(array.shape)
    shape[axis] //= 2
    half = shape[axis]

    def body(place_ref, ref, kept, sent):
        mine = (place_ref[0] >> bit) & 1
        for out, at in ((kept, mine), (sent, 1 - mine)):
            rows = pl.ds(pl.multiple_of(at * half, half), half)
            out[...] = ref[rows, :] if axis == 0 else ref[:, rows]

    outs = [jax.ShapeDtypeStruct(tuple(shape), array.dtype)] * 2
    return kernel_call(body, outs, [place, array], name)


def packed(k, v, name):
    tokens, width = k.shape

    def body(k_ref, v_ref, out, done):
        copies = [
            pltpu.make_async_copy(ref, out.at[:, pl.ds(at, width)], done.at[i])
            for i, (ref, at) in enumerate(((k_ref, 0), (v_ref, width)))
        ]
        for copy in copies:
            copy.start()
        for copy in copies:
            copy.wait()

    return pl.pallas_call(
        body,
        out_shape=pltpu.VMEM((tokens, 2 * width), k.dtype),
        in_specs=[pl.BlockSpec(memory_space=pl.ANY)] * 2,
        out_specs=VMEM,
        scratch_shapes=[pltpu.SemaphoreType.DMA((2,))],
        cost_estimate=COST,
        name=name,
    )(k, v)


def quarters(state, place, name):
    rows = state.shape[0] // 4

    def body(place_ref, ref, *outs):
        mine = place_ref[0] & 3
        for step, out in enumerate(outs):
            at = pl.multiple_of((mine ^ step) * rows, rows)
            out[...] = ref[pl.ds(at, rows), :]

    outs = [jax.ShapeDtypeStruct((rows, state.shape[1]), state.dtype)] * 4
    return kernel_call(body, outs, [place, state], name)


def added(arrays, name):
    def body(*refs):
        total = functools.reduce(jnp.add, [ref[...].astype(jnp.float32) for ref in refs[:-1]])
        refs[-1][...] = total.astype(refs[-1].dtype)

    outs = [jax.ShapeDtypeStruct(arrays[0].shape, arrays[0].dtype)]
    return kernel_call(body, outs, list(arrays), name)[0]


def whole_state(parts, place, name):
    rows = parts[0].shape[0]

    def body(place_ref, *refs):
        mine = place_ref[0] & 3
        for step, ref in enumerate(refs[:-1]):
            at = pl.multiple_of((mine ^ step) * rows, rows)
            refs[-1][pl.ds(at, rows), :] = ref[...]

    outs = [jax.ShapeDtypeStruct((4 * rows, parts[0].shape[1]), parts[0].dtype)]
    return kernel_call(body, outs, [place] + list(parts), name)[0]


def swapped(shard, axis, distance):
    return lax.ppermute(shard, axis, [(i, i ^ distance) for i in range(lax.axis_size(axis))])


def moved(shard, steps):
    span = lax.axis_size("seq") // 4
    return lax.ppermute(
        shard, "seq", [(a * span + r, b * span + r) for a, b in steps for r in range(span)]
    )


def every_distance(q, k, v, feat, w):
    index = lax.axis_index("seq").astype(jnp.int32).reshape(1)
    core = lax.axis_index("head").astype(jnp.int32).reshape(1)
    width = q.shape[1]

    first_steps = [(1, 3), (2, 0), (0, 1), (3, 2)]
    second_steps = [(1, 2), (2, 1)]
    edge_steps = [(1, 0), (2, 3)]
    after = lax.optimization_barrier
    pairs = width // PAIR
    split = pairs // 2 * PAIR

    k, index, core = after((k, index, core))
    k_1 = moved(k, first_steps)
    state = key_state(whole(k), whole(v), feat, pairs)
    kept, *sent = quarters(state, index, "state_quarters")
    got = [swapped(part, "seq", d) for part, d in zip(sent, (1, 2, 3))]
    got, k_next, v_next = after((got, k, v))
    v_1 = moved(v_next, first_steps)
    k_near = [swapped(k_next, "seq", d) for d in (1, 2)]
    state = added([kept] + got, "state_plane")
    state, k_1 = after((state, k_1))
    got = swapped(state, "seq", 4)
    sums = attend(q, [(whole(k), whole(v))], None, "attend_own")
    first = weigh(q, [[whole(k_1)]], "weigh_first")
    first, w = after((first, w))
    w_own, w_sent = parted(w, core, 0, 1, "weights_parted")
    w_far = swapped(w_sent, "head", 1)

    got, k_1, k_near, v_1, w_far, sums, k_next, v_next = after(
        (got, k_1, k_near, v_1, w_far, sums, k, v)
    )
    state = added([state, got], "state_line")
    got = swapped(state, "seq", 8)
    k_2 = moved(k_1, second_steps)
    k_3 = moved(k_next, edge_steps)
    v_near = [swapped(v_next, "seq", d) for d in (1, 2)]
    everyone = range(pairs)
    sums = gather(sums, first, [[whole(v_1)]], None, everyone, "gather_first")
    near = weigh(q, [[whole(far)] for far in k_near], "weigh_near")

    got, v_1, v_last, near, sums = after((got, v_1, v, near, sums))
    v_2 = moved(v_1, second_steps)
    v_3 = moved(v_last, edge_steps)
    v_near, got, sums, near, k_2, k_3 = after((v_near, got, sums, near, k_2, k_3))
    last = weigh(q, [[whole(k_2), whole(k_3)]], "weigh_last")
    state = added([state, got], "state_summed")
    got = [swapped(state, "seq", d) for d in (1, 2, 3)]
    sums = gather(sums, near, [[whole(far)] for far in v_near], None, everyone, "gather_near")
    got, sums, last = after((got, sums, last))
    state = whole_state([state] + got, index, "state_whole")
    low = low_rank_rows(q, feat, state)

    v_last = [[whole(v_2), whole(v_3)]]
    rows_a = gather(sums, last, v_last, low, range(0, pairs // 2), "gather_a")
    far_a = swapped(rows_a, "head", 1)
    rows_b = gather(sums, last, v_last, low, range(pairs // 2, pairs), "gather_b")
    far_b = swapped(rows_b, "head", 1)
    acc = project(None, [(rows_a, w_own, 0), (far_a, w_far, 0), (rows_b, w_own, split)], "project_a")
    return project(acc, [(far_b, w_far, split)], "project_b")


def chosen_distances(q, k, v, distances, feat, w):
    state = key_state(whole(k), whole(v), feat, q.shape[1] // PAIR).astype(jnp.float32)
    state = lax.psum(state, "seq").astype(jnp.bfloat16)
    bits = lax.axis_size("seq").bit_length() - 1
    bit_ids = jnp.arange(bits, dtype=jnp.int32)
    powers = jnp.left_shift(jnp.ones((bits,), jnp.int32), bit_ids)

    def path(bit):
        return lambda pair: (swapped(pair[0], "seq", 1 << bit), swapped(pair[1], "seq", 1 << bit))

    paths = [path(bit) for bit in range(bits)]
    low = low_rank_rows(q, feat, state)
    sums = attend(q, [(whole(k), whole(v))], None, "attend_own")
    for partner in range(PARTNERS):
        picked = jnp.sum(jnp.where(distances[partner] == powers, bit_ids, 0))
        far = [whole(x) for x in lax.switch(picked, paths, (k, v))]
        if partner < PARTNERS - 1:
            sums = attend(q, [far], sums, "attend_far")
    rows = finish(q, [far], sums, low, range(q.shape[1] // PAIR), "finish")
    part = jnp.dot(rows, w, preferred_element_type=jnp.float32)
    return lax.psum_scatter(part.astype(jnp.bfloat16), "head", scatter_dimension=1, tiled=True)


def per_device(queries, keys, values, distances, feature_proj, out_proj):
    if lax.axis_size("seq") == 1 << PARTNERS and lax.axis_size("head") == 2:
        return every_distance(queries, keys, values, feature_proj, out_proj)
    return chosen_distances(queries, keys, values, distances, feature_proj, out_proj)


def solution(mesh):
    in_specs = (P("seq", "head"), P("seq", "head"), P("seq", "head"), P(), P(), P("head", None))
    return jax.shard_map(
        per_device, mesh=mesh, in_specs=in_specs, out_specs=P("seq", "head"), check_vma=False
    )
```

```python
import functools

import jax
import jax.numpy as jnp
from jax import lax
from jax.experimental import pallas as pl
from jax.experimental.pallas import tpu as pltpu
from jax.sharding import PartitionSpec as P

HEAD_DIM = 64
PARTNERS = 4
PAIR = 2 * HEAD_DIM
NT = (((1,), (1,)), ((), ()))
VMEM = pl.BlockSpec(memory_space=pltpu.VMEM)
SMEM = pl.BlockSpec(memory_space=pltpu.SMEM)
VMEM_LIMIT = 20 * 2**20
COST = pl.CostEstimate(flops=1000, transcendentals=0, bytes_accessed=0)


def low_lanes(rows):
    return lax.broadcasted_iota(jnp.int32, (rows, PAIR), 1) < HEAD_DIM


def half_of(pair, half, other):
    low = low_lanes(pair.shape[0])
    fill = jnp.full_like(pair, other)
    return jnp.where(low, pair, fill) if half == 0 else jnp.where(low, fill, pair)


def cols(ref, c):
    return ref[:, c * PAIR:(c + 1) * PAIR]


def block_of(refs):
    return functools.reduce(jnp.add, [ref[...] for ref in refs])


def weigh_head(q_pair, k_pairs, half):
    q_one = half_of(q_pair, half, 0)
    scores = [lax.dot_general(q_one, k, NT, preferred_element_type=jnp.float32) for k in k_pairs]
    top = functools.reduce(jnp.maximum, [jnp.max(s, axis=-1, keepdims=True) for s in scores])
    return top, [jnp.exp(s - top).astype(jnp.bfloat16) for s in scores]


def scaled(q_pair):
    return q_pair * jnp.asarray(HEAD_DIM ** -0.5, q_pair.dtype)


def add_values(weights, v_pairs, half):
    parts = [
        jnp.dot(w, half_of(v, half, 1), preferred_element_type=jnp.float32)
        for w, v in zip(weights, v_pairs)
    ]
    return functools.reduce(jnp.add, parts)


def numer_denom(first, second):
    low = low_lanes(first.shape[0])
    denom = pltpu.roll(jnp.where(low, second, first), HEAD_DIM, 1)
    return jnp.where(low, first, second), denom


def joined(states):
    top = functools.reduce(jnp.maximum, [t for t, _, _ in states])
    factors = [jnp.exp(t - top) for t, _, _ in states]
    numer = functools.reduce(jnp.add, [n * f for (_, n, _), f in zip(states, factors)])
    denom = functools.reduce(jnp.add, [d * f for (_, _, d), f in zip(states, factors)])
    return top, numer, denom


def kernel_call(body, outs, args, name):
    return pl.pallas_call(
        body,
        out_shape=[pltpu.VMEM(o.shape, o.dtype) for o in outs],
        in_specs=[SMEM if a.dtype == jnp.int32 else VMEM for a in args],
        out_specs=[VMEM] * len(outs),
        compiler_params=pltpu.CompilerParams(vmem_limit_bytes=VMEM_LIMIT),
        cost_estimate=COST,
        name=name,
    )(*args)


def whole(array):
    return [(array, 0, array.shape[1])]


def pairs_call(body, outs, operands, pairs, total, name):
    arrays, places = [], {}
    for c in pairs:
        for number, operand in enumerate(operands):
            share = sum(count for _, _, count in operand) // total
            at = c * share
            for array, first, count in operand:
                if 0 <= at < count:
                    if not any(array is other for other in arrays):
                        arrays.append(array)
                    index = [array is other for other in arrays].index(True)
                    places[c, number] = index, slice(first + at, first + at + share)
                at -= count

    def every_pair(*refs):
        for c in pairs:
            spots = [places[c, number] for number in range(len(operands))]
            ins = [refs[index].at[:, part] for index, part in spots]
            results = []
            for ref in refs[len(arrays):]:
                share = ref.shape[1] // len(pairs)
                at = (c - pairs.start) * share
                results.append(ref.at[:, at:at + share])
            body(*ins, *results)

    return kernel_call(every_pair, outs, arrays, name)


def attend(q, blocks, before, name):
    tokens, width = q.shape
    operands = [whole(q)] + [x for block in blocks for x in block]
    count = len(operands)
    operands += [whole(x) for x in before or []]

    def body(*refs):
        outs = refs[-3:]
        q_pair = scaled(refs[0][...])
        k_pairs = [r[...] for r in refs[1:count:2]]
        v_pairs = [r[...] for r in refs[2:count:2]]
        tops, sums = [], []
        for half in range(2):
            top, weights = weigh_head(q_pair, k_pairs, half)
            tops.append(top)
            sums.append(add_values(weights, v_pairs, half))
        state = (jnp.where(low_lanes(tokens), *tops), *numer_denom(*sums))
        if before is not None:
            state = joined([state, tuple(r[...] for r in refs[count:-3])])
        for out, value in zip(outs, state):
            out[...] = value

    outs = [jax.ShapeDtypeStruct((tokens, width), jnp.float32)] * 3
    return pairs_call(body, outs, operands, range(width // PAIR), width // PAIR, name)


def weigh(q, blocks, name):
    tokens, width = q.shape
    keys = blocks[0][0][0][0].shape[0]
    count = len(blocks)

    def body(q_ref, *refs):
        w_out, top_out = refs[-2:]
        q_pair = scaled(q_ref[...])
        rest = list(refs[:-2])
        k_pairs = [block_of([rest.pop(0) for _ in block]) for block in blocks]
        tops = []
        for half in range(2):
            top, weights = weigh_head(q_pair, k_pairs, half)
            tops.append(top)
            for i, w in enumerate(weights):
                at = (half * count + i) * keys
                w_out[:, at:at + keys] = w
        top_out[...] = jnp.where(low_lanes(tokens), *tops)

    outs = [
        jax.ShapeDtypeStruct((tokens, width // HEAD_DIM * count * keys), jnp.bfloat16),
        jax.ShapeDtypeStruct((tokens, width), jnp.float32),
    ]
    operands = [whole(q)] + [part for block in blocks for part in block]
    return pairs_call(body, outs, operands, range(width // PAIR), width // PAIR, name)


def gather(before, weighed, blocks, low_rank, pairs, name):
    weights, tops = weighed
    tokens, width = tops.shape
    count = len(blocks)
    keys = weights.shape[1] // (width // HEAD_DIM) // count
    operands = [whole(x) for x in (*before, weights, tops)]
    operands += [part for block in blocks for part in block]
    if low_rank is not None:
        operands.append(whole(low_rank))

    def body(*refs):
        rest = list(refs[5:len(operands)])
        v_pairs = [block_of([rest.pop(0) for _ in block]) for block in blocks]
        sums = []
        for half in range(2):
            ats = [(half * count + i) * keys for i in range(count)]
            sums.append(add_values([refs[3][:, at:at + keys] for at in ats], v_pairs, half))
        state = joined([tuple(r[...] for r in refs[:3]), (refs[4][...], *numer_denom(*sums))])
        if low_rank is not None:
            state = [(state[1] / state[2] + rest[0][...]).astype(jnp.bfloat16)]
        for out, value in zip(refs[len(operands):], state):
            out[...] = value

    if low_rank is not None:
        outs = [jax.ShapeDtypeStruct((tokens, len(pairs) * PAIR), jnp.bfloat16)]
        return pairs_call(body, outs, operands, pairs, width // PAIR, name)[0]
    outs = [jax.ShapeDtypeStruct((tokens, width), jnp.float32)] * 3
    return pairs_call(body, outs, operands, pairs, width // PAIR, name)


def finish(q, parts, before, low_rank, pairs, name):
    tokens, width = q.shape
    count = len(parts)
    operands = [whole(q)] + [k for k, _ in parts] + [v for _, v in parts]
    operands += [whole(x) for x in (*before, low_rank)]

    def body(*refs):
        q_pair = scaled(refs[0][...])
        k_pair, v_pair = block_of(refs[1:1 + count]), block_of(refs[1 + count:1 + 2 * count])
        tops, sums = [], []
        for half in range(2):
            top, weights = weigh_head(q_pair, [k_pair], half)
            tops.append(top)
            sums.append(add_values(weights, [v_pair], half))
        state = (jnp.where(low_lanes(tokens), *tops), *numer_denom(*sums))
        _, numer, denom = joined([state, tuple(r[...] for r in refs[1 + 2 * count:-2])])
        refs[-1][...] = (numer / denom + refs[-2][...]).astype(jnp.bfloat16)

    outs = [jax.ShapeDtypeStruct((tokens, len(pairs) * PAIR), jnp.bfloat16)]
    return pairs_call(body, outs, operands, pairs, width // PAIR, name)[0]


def twice(feat):
    return jnp.concatenate([feat, feat], axis=0)


def state_rows(pairs, features):
    return pairs * features + features


def key_state(k, v, feat, pairs):
    features = feat.shape[1]
    spread = PAIR // (2 * pairs)
    arrays = []
    for array, _, _ in k + v:
        if not any(array is other for other in arrays):
            arrays.append(array)

    def pair_of(refs, operand, c):
        at = c * PAIR
        for array, first, count in operand:
            if 0 <= at < count:
                index = [array is other for other in arrays].index(True)
                return refs[index][:, first + at:first + at + PAIR]
            at -= count

    def body(*refs):
        feat_ref, out = refs[-2:]
        feat_t = twice(feat_ref[...].astype(jnp.float32)).T.astype(jnp.bfloat16)
        lane = lax.broadcasted_iota(jnp.int32, (features, PAIR), 1)
        norms = jnp.zeros((features, PAIR), jnp.float32)
        for c in range(pairs):
            k_pair, v_pair = pair_of(refs, k, c), pair_of(refs, v, c)
            k_float = k_pair.astype(jnp.float32)
            square = k_float * k_float
            square_hi = square.astype(jnp.bfloat16)
            square_lo = (square - square_hi.astype(jnp.float32)).astype(jnp.bfloat16)
            parts = []
            for half in range(2):
                proj = lax.dot_general(
                    half_of(feat_t, half, 0), k_pair, NT, preferred_element_type=jnp.float32
                )
                ones = half_of(jnp.ones((16, PAIR), jnp.bfloat16), half, 0)
                size = lax.dot_general(ones, square_hi, NT, preferred_element_type=jnp.float32)
                size += lax.dot_general(ones, square_lo, NT, preferred_element_type=jnp.float32)
                phi = jnp.exp(
                    proj * HEAD_DIM ** -0.25 - size[0:1, :] * (0.5 * HEAD_DIM ** -0.5)
                ).astype(jnp.bfloat16)
                parts.append(
                    jnp.dot(phi, half_of(v_pair, half, 1), preferred_element_type=jnp.float32)
                )
            out[c * features:(c + 1) * features, :] = jnp.where(
                low_lanes(features), parts[0], parts[1]
            ).astype(jnp.bfloat16)
            for half in range(2):
                at = (2 * c + half) * spread
                column = parts[half][:, (1 - half) * HEAD_DIM:(1 - half) * HEAD_DIM + 1]
                norms = jnp.where((lane >= at) & (lane < at + spread), column, norms)
        out[pairs * features:, :] = norms.astype(jnp.bfloat16)

    outs = jax.ShapeDtypeStruct((state_rows(pairs, features), PAIR), jnp.bfloat16)
    return kernel_call(body, [outs], arrays + [feat], "key_state")[0]


def low_rank_rows(q, feat, state):
    tokens, width = q.shape
    pairs, features = width // PAIR, feat.shape[1]
    spread = PAIR // (2 * pairs)

    def body(q_ref, feat_ref, state_ref, out):
        feat_two = twice(feat_ref[...])
        norms = state_ref[pairs * features:, :]
        for c in range(pairs):
            q_pair = cols(q_ref, c)
            kv = state_ref[c * features:(c + 1) * features, :]
            low = low_lanes(features)
            parts = []
            for half in range(2):
                proj = jnp.dot(
                    half_of(q_pair, half, 0), feat_two, preferred_element_type=jnp.float32
                ) * HEAD_DIM ** -0.25
                phi = jnp.exp(proj - jnp.max(proj, axis=-1, keepdims=True)).astype(jnp.bfloat16)
                at = (2 * c + half) * spread
                column = jnp.broadcast_to(norms[:, at:at + 1], kv.shape)
                both = jnp.where(low, kv, column) if half == 0 else jnp.where(low, column, kv)
                parts.append(jnp.dot(phi, both, preferred_element_type=jnp.float32))
            numer, denom = numer_denom(*parts)
            out[:, c * PAIR:(c + 1) * PAIR] = numer / denom

    outs = jax.ShapeDtypeStruct((tokens, width), jnp.float32)
    return kernel_call(body, [outs], [q, feat, state], "low_rank")[0]


def project(acc, parts, name):
    tokens, width = parts[0][0].shape[0], parts[0][1].shape[1]
    arrays = []
    for array in [x for rows, w, _ in parts for x in (rows, w)] + ([] if acc is None else [acc]):
        if not any(array is other for other in arrays):
            arrays.append(array)

    def body(*refs):
        def ref_of(array):
            return refs[[array is other for other in arrays].index(True)]

        total = None if acc is None else ref_of(acc)[...]
        for rows, w, first in parts:
            w_rows = ref_of(w)[first:first + rows.shape[1], :]
            part = jnp.dot(ref_of(rows)[...], w_rows, preferred_element_type=jnp.float32)
            total = part if total is None else total + part
        refs[-1][...] = total.astype(refs[-1].dtype)

    if acc is None:
        outs = [jax.ShapeDtypeStruct((tokens, width), jnp.float32)]
        return kernel_call(body, outs, arrays, name)[0]
    return pl.pallas_call(
        body,
        out_shape=jax.ShapeDtypeStruct((tokens, width), jnp.bfloat16),
        in_specs=[VMEM] * len(arrays),
        out_specs=VMEM,
        compiler_params=pltpu.CompilerParams(vmem_limit_bytes=VMEM_LIMIT),
        cost_estimate=COST,
        name=name,
    )(*arrays)


def parted(array, place, bit, axis, name):
    shape = list(array.shape)
    shape[axis] //= 2
    half = shape[axis]

    def body(place_ref, ref, kept, sent):
        mine = (place_ref[0] >> bit) & 1
        for out, at in ((kept, mine), (sent, 1 - mine)):
            rows = pl.ds(pl.multiple_of(at * half, half), half)
            out[...] = ref[rows, :] if axis == 0 else ref[:, rows]

    outs = [jax.ShapeDtypeStruct(tuple(shape), array.dtype)] * 2
    return kernel_call(body, outs, [place, array], name)


def packed(k, v, name):
    tokens, width = k.shape

    def body(k_ref, v_ref, out, done):
        copies = [
            pltpu.make_async_copy(ref, out.at[:, pl.ds(at, width)], done.at[i])
            for i, (ref, at) in enumerate(((k_ref, 0), (v_ref, width)))
        ]
        for copy in copies:
            copy.start()
        for copy in copies:
            copy.wait()

    return pl.pallas_call(
        body,
        out_shape=pltpu.VMEM((tokens, 2 * width), k.dtype),
        in_specs=[pl.BlockSpec(memory_space=pl.ANY)] * 2,
        out_specs=VMEM,
        scratch_shapes=[pltpu.SemaphoreType.DMA((2,))],
        cost_estimate=COST,
        name=name,
    )(k, v)


def quarters(state, place, name):
    rows = state.shape[0] // 4

    def body(place_ref, ref, *outs):
        mine = place_ref[0] & 3
        for step, out in enumerate(outs):
            at = pl.multiple_of((mine ^ step) * rows, rows)
            out[...] = ref[pl.ds(at, rows), :]

    outs = [jax.ShapeDtypeStruct((rows, state.shape[1]), state.dtype)] * 4
    return kernel_call(body, outs, [place, state], name)


def added(arrays, name):
    def body(*refs):
        total = functools.reduce(jnp.add, [ref[...].astype(jnp.float32) for ref in refs[:-1]])
        refs[-1][...] = total.astype(refs[-1].dtype)

    outs = [jax.ShapeDtypeStruct(arrays[0].shape, arrays[0].dtype)]
    return kernel_call(body, outs, list(arrays), name)[0]


def whole_state(parts, place, name):
    rows = parts[0].shape[0]

    def body(place_ref, *refs):
        mine = place_ref[0] & 3
        for step, ref in enumerate(refs[:-1]):
            at = pl.multiple_of((mine ^ step) * rows, rows)
            refs[-1][pl.ds(at, rows), :] = ref[...]

    outs = [jax.ShapeDtypeStruct((4 * rows, parts[0].shape[1]), parts[0].dtype)]
    return kernel_call(body, outs, [place] + list(parts), name)[0]


def swapped(shard, axis, distance):
    return lax.ppermute(shard, axis, [(i, i ^ distance) for i in range(lax.axis_size(axis))])


def moved(shard, steps):
    span = lax.axis_size("seq") // 4
    return lax.ppermute(
        shard, "seq", [(a * span + r, b * span + r) for a, b in steps for r in range(span)]
    )


def every_distance(q, k, v, feat, w):
    index = lax.axis_index("seq").astype(jnp.int32).reshape(1)
    core = lax.axis_index("head").astype(jnp.int32).reshape(1)
    width = q.shape[1]

    first_steps = [(1, 3), (2, 0), (0, 1), (3, 2)]
    second_steps = [(1, 2), (2, 1)]
    edge_steps = [(1, 0), (2, 3)]
    after = lax.optimization_barrier
    pairs = width // PAIR
    split = pairs // 2 * PAIR

    k, index, core = after((k, index, core))
    k_1 = moved(k, first_steps)
    state = key_state(whole(k), whole(v), feat, pairs)
    kept, *sent = quarters(state, index, "state_quarters")
    got = [swapped(part, "seq", d) for part, d in zip(sent, (1, 2, 3))]
    got, k_next, v_next = after((got, k, v))
    v_1 = moved(v_next, first_steps)
    k_near = [swapped(k_next, "seq", d) for d in (1, 2)]
    state = added([kept] + got, "state_plane")
    state, k_1 = after((state, k_1))
    got = swapped(state, "seq", 4)
    sums = attend(q, [(whole(k), whole(v))], None, "attend_own")
    first = weigh(q, [[whole(k_1)]], "weigh_first")
    first, w, v_next = after((first, w, v))
    v_near = swapped(v_next, "seq", 1)
    w_own, w_sent = parted(w, core, 0, 1, "weights_parted")

    got, k_1, v_1, w_sent, sums, k_next, v_next = after((got, k_1, v_1, w_sent, sums, k, v))
    state = added([state, got], "state_line")
    got = swapped(state, "seq", 8)
    k_2 = moved(k_1, second_steps)
    k_3 = moved(k_next, edge_steps)
    v_last = swapped(v_next, "seq", 2)
    everyone = range(pairs)
    sums = gather(sums, first, [[whole(v_1)]], None, everyone, "gather_first")
    near = weigh(q, [[whole(far)] for far in k_near], "weigh_near")

    got, v_1 = after((got, v_1))
    v_2 = moved(v_1, second_steps)
    v_next, near, sums, v_near = after((v, near, sums, v_near))
    v_3 = moved(v_next, edge_steps)
    v_near = [v_near, v_last]
    v_near, got, sums, near, k_2, k_3 = after((v_near, got, sums, near, k_2, k_3))
    last = weigh(q, [[whole(k_2), whole(k_3)]], "weigh_last")
    state = added([state, got], "state_summed")
    got = [swapped(state, "seq", d) for d in (1, 2, 3)]
    sums = gather(sums, near, [[whole(far)] for far in v_near], None, everyone, "gather_near")
    got, sums, last, w_sent = after((got, sums, last, w_sent))
    w_far = swapped(w_sent, "head", 1)
    state = whole_state([state] + got, index, "state_whole")
    low = low_rank_rows(q, feat, state)

    v_last = [[whole(v_2), whole(v_3)]]
    rows_a = gather(sums, last, v_last, low, range(0, pairs // 2), "gather_a")
    far_a = swapped(rows_a, "head", 1)
    rows_b = gather(sums, last, v_last, low, range(pairs // 2, pairs), "gather_b")
    far_b = swapped(rows_b, "head", 1)
    acc = project(None, [(rows_a, w_own, 0), (far_a, w_far, 0), (rows_b, w_own, split)], "project_a")
    return project(acc, [(far_b, w_far, split)], "project_b")


def chosen_distances(q, k, v, distances, feat, w):
    state = key_state(whole(k), whole(v), feat, q.shape[1] // PAIR).astype(jnp.float32)
    state = lax.psum(state, "seq").astype(jnp.bfloat16)
    bits = lax.axis_size("seq").bit_length() - 1
    bit_ids = jnp.arange(bits, dtype=jnp.int32)
    powers = jnp.left_shift(jnp.ones((bits,), jnp.int32), bit_ids)

    def path(bit):
        return lambda pair: (swapped(pair[0], "seq", 1 << bit), swapped(pair[1], "seq", 1 << bit))

    paths = [path(bit) for bit in range(bits)]
    low = low_rank_rows(q, feat, state)
    sums = attend(q, [(whole(k), whole(v))], None, "attend_own")
    for partner in range(PARTNERS):
        picked = jnp.sum(jnp.where(distances[partner] == powers, bit_ids, 0))
        far = [whole(x) for x in lax.switch(picked, paths, (k, v))]
        if partner < PARTNERS - 1:
            sums = attend(q, [far], sums, "attend_far")
    rows = finish(q, [far], sums, low, range(q.shape[1] // PAIR), "finish")
    part = jnp.dot(rows, w, preferred_element_type=jnp.float32)
    return lax.psum_scatter(part.astype(jnp.bfloat16), "head", scatter_dimension=1, tiled=True)


def per_device(queries, keys, values, distances, feature_proj, out_proj):
    if lax.axis_size("seq") == 1 << PARTNERS and lax.axis_size("head") == 2:
        return every_distance(queries, keys, values, feature_proj, out_proj)
    return chosen_distances(queries, keys, values, distances, feature_proj, out_proj)


def solution(mesh):
    in_specs = (P("seq", "head"), P("seq", "head"), P("seq", "head"), P(), P(), P("head", None))
    return jax.shard_map(
        per_device, mesh=mesh, in_specs=in_specs, out_specs=P("seq", "head"), check_vma=False
    )
```

```python
import functools

import jax
import jax.numpy as jnp
from jax import lax
from jax.experimental import pallas as pl
from jax.experimental.pallas import tpu as pltpu
from jax.sharding import PartitionSpec as P

HEAD_DIM = 64
PARTNERS = 4
PAIR = 2 * HEAD_DIM
NT = (((1,), (1,)), ((), ()))
VMEM = pl.BlockSpec(memory_space=pltpu.VMEM)
SMEM = pl.BlockSpec(memory_space=pltpu.SMEM)
VMEM_LIMIT = 20 * 2**20
COST = pl.CostEstimate(flops=1000, transcendentals=0, bytes_accessed=0)


def low_lanes(rows):
    return lax.broadcasted_iota(jnp.int32, (rows, PAIR), 1) < HEAD_DIM


def half_of(pair, half, other):
    low = low_lanes(pair.shape[0])
    fill = jnp.full_like(pair, other)
    return jnp.where(low, pair, fill) if half == 0 else jnp.where(low, fill, pair)


def cols(ref, c):
    return ref[:, c * PAIR:(c + 1) * PAIR]


def block_of(refs):
    return functools.reduce(jnp.add, [ref[...] for ref in refs])


def weigh_head(q_pair, k_pairs, half):
    q_one = half_of(q_pair, half, 0)
    scores = [lax.dot_general(q_one, k, NT, preferred_element_type=jnp.float32) for k in k_pairs]
    top = functools.reduce(jnp.maximum, [jnp.max(s, axis=-1, keepdims=True) for s in scores])
    return top, [jnp.exp(s - top).astype(jnp.bfloat16) for s in scores]


def scaled(q_pair):
    return q_pair * jnp.asarray(HEAD_DIM ** -0.5, q_pair.dtype)


def add_values(weights, v_pairs, half):
    parts = [
        jnp.dot(w, half_of(v, half, 1), preferred_element_type=jnp.float32)
        for w, v in zip(weights, v_pairs)
    ]
    return functools.reduce(jnp.add, parts)


def numer_denom(first, second):
    low = low_lanes(first.shape[0])
    denom = pltpu.roll(jnp.where(low, second, first), HEAD_DIM, 1)
    return jnp.where(low, first, second), denom


def joined(states):
    top = functools.reduce(jnp.maximum, [t for t, _, _ in states])
    factors = [jnp.exp(t - top) for t, _, _ in states]
    numer = functools.reduce(jnp.add, [n * f for (_, n, _), f in zip(states, factors)])
    denom = functools.reduce(jnp.add, [d * f for (_, _, d), f in zip(states, factors)])
    return top, numer, denom


def kernel_call(body, outs, args, name):
    return pl.pallas_call(
        body,
        out_shape=[pltpu.VMEM(o.shape, o.dtype) for o in outs],
        in_specs=[SMEM if a.dtype == jnp.int32 else VMEM for a in args],
        out_specs=[VMEM] * len(outs),
        compiler_params=pltpu.CompilerParams(vmem_limit_bytes=VMEM_LIMIT),
        cost_estimate=COST,
        name=name,
    )(*args)


def whole(array):
    return [(array, 0, array.shape[1])]


def pairs_call(body, outs, operands, pairs, total, name):
    arrays, places = [], {}
    for c in pairs:
        for number, operand in enumerate(operands):
            share = sum(count for _, _, count in operand) // total
            at = c * share
            for array, first, count in operand:
                if 0 <= at < count:
                    if not any(array is other for other in arrays):
                        arrays.append(array)
                    index = [array is other for other in arrays].index(True)
                    places[c, number] = index, slice(first + at, first + at + share)
                at -= count

    def every_pair(*refs):
        for c in pairs:
            spots = [places[c, number] for number in range(len(operands))]
            ins = [refs[index].at[:, part] for index, part in spots]
            results = []
            for ref in refs[len(arrays):]:
                share = ref.shape[1] // len(pairs)
                at = (c - pairs.start) * share
                results.append(ref.at[:, at:at + share])
            body(*ins, *results)

    return kernel_call(every_pair, outs, arrays, name)


def attend(q, blocks, before, name):
    tokens, width = q.shape
    operands = [whole(q)] + [x for block in blocks for x in block]
    count = len(operands)
    operands += [whole(x) for x in before or []]

    def body(*refs):
        outs = refs[-3:]
        q_pair = scaled(refs[0][...])
        k_pairs = [r[...] for r in refs[1:count:2]]
        v_pairs = [r[...] for r in refs[2:count:2]]
        tops, sums = [], []
        for half in range(2):
            top, weights = weigh_head(q_pair, k_pairs, half)
            tops.append(top)
            sums.append(add_values(weights, v_pairs, half))
        state = (jnp.where(low_lanes(tokens), *tops), *numer_denom(*sums))
        if before is not None:
            state = joined([state, tuple(r[...] for r in refs[count:-3])])
        for out, value in zip(outs, state):
            out[...] = value

    outs = [jax.ShapeDtypeStruct((tokens, width), jnp.float32)] * 3
    return pairs_call(body, outs, operands, range(width // PAIR), width // PAIR, name)


def weigh(q, blocks, name):
    tokens, width = q.shape
    keys = blocks[0][0][0][0].shape[0]
    count = len(blocks)

    def body(q_ref, *refs):
        w_out, top_out = refs[-2:]
        q_pair = scaled(q_ref[...])
        rest = list(refs[:-2])
        k_pairs = [block_of([rest.pop(0) for _ in block]) for block in blocks]
        tops = []
        for half in range(2):
            top, weights = weigh_head(q_pair, k_pairs, half)
            tops.append(top)
            for i, w in enumerate(weights):
                at = (half * count + i) * keys
                w_out[:, at:at + keys] = w
        top_out[...] = jnp.where(low_lanes(tokens), *tops)

    outs = [
        jax.ShapeDtypeStruct((tokens, width // HEAD_DIM * count * keys), jnp.bfloat16),
        jax.ShapeDtypeStruct((tokens, width), jnp.float32),
    ]
    operands = [whole(q)] + [part for block in blocks for part in block]
    return pairs_call(body, outs, operands, range(width // PAIR), width // PAIR, name)


def gather(before, weighed, blocks, low_rank, pairs, name):
    weights, tops = weighed
    tokens, width = tops.shape
    count = len(blocks)
    keys = weights.shape[1] // (width // HEAD_DIM) // count
    operands = [whole(x) for x in (*before, weights, tops)]
    operands += [part for block in blocks for part in block]
    if low_rank is not None:
        operands.append(whole(low_rank))

    def body(*refs):
        rest = list(refs[5:len(operands)])
        v_pairs = [block_of([rest.pop(0) for _ in block]) for block in blocks]
        sums = []
        for half in range(2):
            ats = [(half * count + i) * keys for i in range(count)]
            sums.append(add_values([refs[3][:, at:at + keys] for at in ats], v_pairs, half))
        state = joined([tuple(r[...] for r in refs[:3]), (refs[4][...], *numer_denom(*sums))])
        if low_rank is not None:
            state = [(state[1] / state[2] + rest[0][...]).astype(jnp.bfloat16)]
        for out, value in zip(refs[len(operands):], state):
            out[...] = value

    if low_rank is not None:
        outs = [jax.ShapeDtypeStruct((tokens, len(pairs) * PAIR), jnp.bfloat16)]
        return pairs_call(body, outs, operands, pairs, width // PAIR, name)[0]
    outs = [jax.ShapeDtypeStruct((tokens, width), jnp.float32)] * 3
    return pairs_call(body, outs, operands, pairs, width // PAIR, name)


def finish(q, parts, before, low_rank, pairs, name):
    tokens, width = q.shape
    count = len(parts)
    operands = [whole(q)] + [k for k, _ in parts] + [v for _, v in parts]
    operands += [whole(x) for x in (*before, low_rank)]

    def body(*refs):
        q_pair = scaled(refs[0][...])
        k_pair, v_pair = block_of(refs[1:1 + count]), block_of(refs[1 + count:1 + 2 * count])
        tops, sums = [], []
        for half in range(2):
            top, weights = weigh_head(q_pair, [k_pair], half)
            tops.append(top)
            sums.append(add_values(weights, [v_pair], half))
        state = (jnp.where(low_lanes(tokens), *tops), *numer_denom(*sums))
        _, numer, denom = joined([state, tuple(r[...] for r in refs[1 + 2 * count:-2])])
        refs[-1][...] = (numer / denom + refs[-2][...]).astype(jnp.bfloat16)

    outs = [jax.ShapeDtypeStruct((tokens, len(pairs) * PAIR), jnp.bfloat16)]
    return pairs_call(body, outs, operands, pairs, width // PAIR, name)[0]


def twice(feat):
    return jnp.concatenate([feat, feat], axis=0)


def state_rows(pairs, features):
    return pairs * features + features


def key_state(k, v, feat, pairs):
    features = feat.shape[1]
    spread = PAIR // (2 * pairs)
    arrays = []
    for array, _, _ in k + v:
        if not any(array is other for other in arrays):
            arrays.append(array)

    def pair_of(refs, operand, c):
        at = c * PAIR
        for array, first, count in operand:
            if 0 <= at < count:
                index = [array is other for other in arrays].index(True)
                return refs[index][:, first + at:first + at + PAIR]
            at -= count

    count = len(arrays) + 1

    def body(*refs):
        out, done = refs[count], refs[-1]
        copies = []
        for c in range(pairs):
            part = pl.ds(c * PAIR, PAIR)
            copies.append([
                pltpu.make_async_copy(refs[i].at[:, part], refs[count + 1 + i].at[:, part], done.at[i, c])
                for i in range(count - 1)
            ])
        copies[0].append(pltpu.make_async_copy(refs[count - 1], refs[2 * count], done.at[count - 1, 0]))
        for group in copies:
            for copy in group:
                copy.start()
        for copy in copies[0]:
            copy.wait()
        refs = refs[count + 1:-1]
        feat_ref = refs[-1]
        feat_t = twice(feat_ref[...].astype(jnp.float32)).T.astype(jnp.bfloat16)
        lane = lax.broadcasted_iota(jnp.int32, (features, PAIR), 1)
        norms = jnp.zeros((features, PAIR), jnp.float32)
        for c in range(pairs):
            for copy in copies[c] if c else []:
                copy.wait()
            k_pair, v_pair = pair_of(refs, k, c), pair_of(refs, v, c)
            k_float = k_pair.astype(jnp.float32)
            square = k_float * k_float
            square_hi = square.astype(jnp.bfloat16)
            square_lo = (square - square_hi.astype(jnp.float32)).astype(jnp.bfloat16)
            parts = []
            for half in range(2):
                proj = lax.dot_general(
                    half_of(feat_t, half, 0), k_pair, NT, preferred_element_type=jnp.float32
                )
                ones = half_of(jnp.ones((16, PAIR), jnp.bfloat16), half, 0)
                size = lax.dot_general(ones, square_hi, NT, preferred_element_type=jnp.float32)
                size += lax.dot_general(ones, square_lo, NT, preferred_element_type=jnp.float32)
                phi = jnp.exp(
                    proj * HEAD_DIM ** -0.25 - size[0:1, :] * (0.5 * HEAD_DIM ** -0.5)
                ).astype(jnp.bfloat16)
                parts.append(
                    jnp.dot(phi, half_of(v_pair, half, 1), preferred_element_type=jnp.float32)
                )
            out[c * features:(c + 1) * features, :] = jnp.where(
                low_lanes(features), parts[0], parts[1]
            ).astype(jnp.bfloat16)
            for half in range(2):
                at = (2 * c + half) * spread
                column = parts[half][:, (1 - half) * HEAD_DIM:(1 - half) * HEAD_DIM + 1]
                norms = jnp.where((lane >= at) & (lane < at + spread), column, norms)
        out[pairs * features:, :] = norms.astype(jnp.bfloat16)

    outs = jax.ShapeDtypeStruct((state_rows(pairs, features), PAIR), jnp.bfloat16)
    args = arrays + [feat]
    return pl.pallas_call(
        body,
        out_shape=pltpu.VMEM(outs.shape, outs.dtype),
        in_specs=[pl.BlockSpec(memory_space=pl.ANY)] * count,
        out_specs=VMEM,
        scratch_shapes=[pltpu.VMEM(x.shape, x.dtype) for x in args]
        + [pltpu.SemaphoreType.DMA((count, pairs))],
        compiler_params=pltpu.CompilerParams(vmem_limit_bytes=VMEM_LIMIT),
        cost_estimate=COST,
        name="key_state",
    )(*args)


def low_rank_rows(q, feat, state):
    tokens, width = q.shape
    pairs, features = width // PAIR, feat.shape[1]
    spread = PAIR // (2 * pairs)

    def body(q_ref, feat_ref, state_ref, out):
        feat_two = twice(feat_ref[...])
        norms = state_ref[pairs * features:, :]
        for c in range(pairs):
            q_pair = cols(q_ref, c)
            kv = state_ref[c * features:(c + 1) * features, :]
            low = low_lanes(features)
            parts = []
            for half in range(2):
                proj = jnp.dot(
                    half_of(q_pair, half, 0), feat_two, preferred_element_type=jnp.float32
                ) * HEAD_DIM ** -0.25
                phi = jnp.exp(proj - jnp.max(proj, axis=-1, keepdims=True)).astype(jnp.bfloat16)
                at = (2 * c + half) * spread
                column = jnp.broadcast_to(norms[:, at:at + 1], kv.shape)
                both = jnp.where(low, kv, column) if half == 0 else jnp.where(low, column, kv)
                parts.append(jnp.dot(phi, both, preferred_element_type=jnp.float32))
            numer, denom = numer_denom(*parts)
            out[:, c * PAIR:(c + 1) * PAIR] = numer / denom

    outs = jax.ShapeDtypeStruct((tokens, width), jnp.float32)
    return kernel_call(body, [outs], [q, feat, state], "low_rank")[0]


def project(acc, parts, name):
    tokens, width = parts[0][0].shape[0], parts[0][1].shape[1]
    arrays = []
    for array in [x for rows, w, _ in parts for x in (rows, w)] + ([] if acc is None else [acc]):
        if not any(array is other for other in arrays):
            arrays.append(array)

    def body(*refs):
        def ref_of(array):
            return refs[[array is other for other in arrays].index(True)]

        total = None if acc is None else ref_of(acc)[...]
        for rows, w, first in parts:
            w_rows = ref_of(w)[first:first + rows.shape[1], :]
            part = jnp.dot(ref_of(rows)[...], w_rows, preferred_element_type=jnp.float32)
            total = part if total is None else total + part
        refs[-1][...] = total.astype(refs[-1].dtype)

    if acc is None:
        outs = [jax.ShapeDtypeStruct((tokens, width), jnp.float32)]
        return kernel_call(body, outs, arrays, name)[0]
    return pl.pallas_call(
        body,
        out_shape=jax.ShapeDtypeStruct((tokens, width), jnp.bfloat16),
        in_specs=[VMEM] * len(arrays),
        out_specs=VMEM,
        compiler_params=pltpu.CompilerParams(vmem_limit_bytes=VMEM_LIMIT),
        cost_estimate=COST,
        name=name,
    )(*arrays)


def parted(array, place, bit, axis, name):
    shape = list(array.shape)
    shape[axis] //= 2
    half = shape[axis]

    def body(place_ref, ref, kept, sent):
        mine = (place_ref[0] >> bit) & 1
        for out, at in ((kept, mine), (sent, 1 - mine)):
            rows = pl.ds(pl.multiple_of(at * half, half), half)
            out[...] = ref[rows, :] if axis == 0 else ref[:, rows]

    outs = [jax.ShapeDtypeStruct(tuple(shape), array.dtype)] * 2
    return kernel_call(body, outs, [place, array], name)


def packed(k, v, name):
    tokens, width = k.shape

    def body(k_ref, v_ref, out, done):
        copies = [
            pltpu.make_async_copy(ref, out.at[:, pl.ds(at, width)], done.at[i])
            for i, (ref, at) in enumerate(((k_ref, 0), (v_ref, width)))
        ]
        for copy in copies:
            copy.start()
        for copy in copies:
            copy.wait()

    return pl.pallas_call(
        body,
        out_shape=pltpu.VMEM((tokens, 2 * width), k.dtype),
        in_specs=[pl.BlockSpec(memory_space=pl.ANY)] * 2,
        out_specs=VMEM,
        scratch_shapes=[pltpu.SemaphoreType.DMA((2,))],
        cost_estimate=COST,
        name=name,
    )(k, v)


def quarters(state, place, name):
    rows = state.shape[0] // 4

    def body(place_ref, ref, *outs):
        mine = place_ref[0] & 3
        for step, out in enumerate(outs):
            at = pl.multiple_of((mine ^ step) * rows, rows)
            out[...] = ref[pl.ds(at, rows), :]

    outs = [jax.ShapeDtypeStruct((rows, state.shape[1]), state.dtype)] * 4
    return kernel_call(body, outs, [place, state], name)


def added(arrays, name):
    def body(*refs):
        total = functools.reduce(jnp.add, [ref[...].astype(jnp.float32) for ref in refs[:-1]])
        refs[-1][...] = total.astype(refs[-1].dtype)

    outs = [jax.ShapeDtypeStruct(arrays[0].shape, arrays[0].dtype)]
    return kernel_call(body, outs, list(arrays), name)[0]


def whole_state(parts, place, name):
    rows = parts[0].shape[0]

    def body(place_ref, *refs):
        mine = place_ref[0] & 3
        for step, ref in enumerate(refs[:-1]):
            at = pl.multiple_of((mine ^ step) * rows, rows)
            refs[-1][pl.ds(at, rows), :] = ref[...]

    outs = [jax.ShapeDtypeStruct((4 * rows, parts[0].shape[1]), parts[0].dtype)]
    return kernel_call(body, outs, [place] + list(parts), name)[0]


def swapped(shard, axis, distance):
    return lax.ppermute(shard, axis, [(i, i ^ distance) for i in range(lax.axis_size(axis))])


def moved(shard, steps):
    span = lax.axis_size("seq") // 4
    return lax.ppermute(
        shard, "seq", [(a * span + r, b * span + r) for a, b in steps for r in range(span)]
    )


def every_distance(q, k, v, feat, w):
    index = lax.axis_index("seq").astype(jnp.int32).reshape(1)
    core = lax.axis_index("head").astype(jnp.int32).reshape(1)
    width = q.shape[1]

    first_steps = [(1, 3), (2, 0), (0, 1), (3, 2)]
    second_steps = [(1, 2), (2, 1)]
    edge_steps = [(1, 0), (2, 3)]
    after = lax.optimization_barrier
    pairs = width // PAIR
    split = pairs // 2 * PAIR

    k, index, core = after((k, index, core))
    k_1 = moved(k, first_steps)
    state = key_state(whole(k), whole(v), feat, pairs)
    kept, *sent = quarters(state, index, "state_quarters")
    got = [swapped(part, "seq", d) for part, d in zip(sent, (1, 2, 3))]
    got, k_next, v_next = after((got, k, v))
    v_1 = moved(v_next, first_steps)
    k_near = [swapped(k_next, "seq", d) for d in (1, 2)]
    state = added([kept] + got, "state_plane")
    state, k_1 = after((state, k_1))
    got = swapped(state, "seq", 4)
    sums = attend(q, [(whole(k), whole(v))], None, "attend_own")
    first = weigh(q, [[whole(k_1)]], "weigh_first")
    first, w, v_next = after((first, w, v))
    v_near = swapped(v_next, "seq", 1)
    w_own, w_sent = parted(w, core, 0, 1, "weights_parted")

    got, k_1, v_1, w_sent, sums, k_next, v_next = after((got, k_1, v_1, w_sent, sums, k, v))
    state = added([state, got], "state_line")
    got = swapped(state, "seq", 8)
    k_2 = moved(k_1, second_steps)
    k_3 = moved(k_next, edge_steps)
    v_last = swapped(v_next, "seq", 2)
    everyone = range(pairs)
    sums = gather(sums, first, [[whole(v_1)]], None, everyone, "gather_first")
    near = weigh(q, [[whole(far)] for far in k_near], "weigh_near")

    got, v_1 = after((got, v_1))
    v_2 = moved(v_1, second_steps)
    v_next, near, sums, v_near = after((v, near, sums, v_near))
    v_3 = moved(v_next, edge_steps)
    v_near = [v_near, v_last]
    v_near, got, sums, near, k_2, k_3 = after((v_near, got, sums, near, k_2, k_3))
    last = weigh(q, [[whole(k_2), whole(k_3)]], "weigh_last")
    state = added([state, got], "state_summed")
    got = [swapped(state, "seq", d) for d in (1, 2, 3)]
    sums = gather(sums, near, [[whole(far)] for far in v_near], None, everyone, "gather_near")
    got, sums, last, w_sent = after((got, sums, last, w_sent))
    w_far = swapped(w_sent, "head", 1)
    state = whole_state([state] + got, index, "state_whole")
    low = low_rank_rows(q, feat, state)

    v_last = [[whole(v_2), whole(v_3)]]
    rows_a = gather(sums, last, v_last, low, range(0, pairs // 2), "gather_a")
    far_a = swapped(rows_a, "head", 1)
    rows_b = gather(sums, last, v_last, low, range(pairs // 2, pairs), "gather_b")
    far_b = swapped(rows_b, "head", 1)
    acc = project(None, [(rows_a, w_own, 0), (far_a, w_far, 0), (rows_b, w_own, split)], "project_a")
    return project(acc, [(far_b, w_far, split)], "project_b")


def chosen_distances(q, k, v, distances, feat, w):
    state = key_state(whole(k), whole(v), feat, q.shape[1] // PAIR).astype(jnp.float32)
    state = lax.psum(state, "seq").astype(jnp.bfloat16)
    bits = lax.axis_size("seq").bit_length() - 1
    bit_ids = jnp.arange(bits, dtype=jnp.int32)
    powers = jnp.left_shift(jnp.ones((bits,), jnp.int32), bit_ids)

    def path(bit):
        return lambda pair: (swapped(pair[0], "seq", 1 << bit), swapped(pair[1], "seq", 1 << bit))

    paths = [path(bit) for bit in range(bits)]
    low = low_rank_rows(q, feat, state)
    sums = attend(q, [(whole(k), whole(v))], None, "attend_own")
    for partner in range(PARTNERS):
        picked = jnp.sum(jnp.where(distances[partner] == powers, bit_ids, 0))
        far = [whole(x) for x in lax.switch(picked, paths, (k, v))]
        if partner < PARTNERS - 1:
            sums = attend(q, [far], sums, "attend_far")
    rows = finish(q, [far], sums, low, range(q.shape[1] // PAIR), "finish")
    part = jnp.dot(rows, w, preferred_element_type=jnp.float32)
    return lax.psum_scatter(part.astype(jnp.bfloat16), "head", scatter_dimension=1, tiled=True)


def per_device(queries, keys, values, distances, feature_proj, out_proj):
    if lax.axis_size("seq") == 1 << PARTNERS and lax.axis_size("head") == 2:
        return every_distance(queries, keys, values, feature_proj, out_proj)
    return chosen_distances(queries, keys, values, distances, feature_proj, out_proj)


def solution(mesh):
    in_specs = (P("seq", "head"), P("seq", "head"), P("seq", "head"), P(), P(), P("head", None))
    return jax.shard_map(
        per_device, mesh=mesh, in_specs=in_specs, out_specs=P("seq", "head"), check_vma=False
    )
```

```python
import functools

import jax
import jax.numpy as jnp
from jax import lax
from jax.experimental import pallas as pl
from jax.experimental.pallas import tpu as pltpu
from jax.sharding import PartitionSpec as P

HEAD_DIM = 64
PARTNERS = 4
PAIR = 2 * HEAD_DIM
NT = (((1,), (1,)), ((), ()))
VMEM = pl.BlockSpec(memory_space=pltpu.VMEM)
SMEM = pl.BlockSpec(memory_space=pltpu.SMEM)
VMEM_LIMIT = 20 * 2**20
COST = pl.CostEstimate(flops=1000, transcendentals=0, bytes_accessed=0)


def low_lanes(rows):
    return lax.broadcasted_iota(jnp.int32, (rows, PAIR), 1) < HEAD_DIM


def half_of(pair, half, other):
    low = low_lanes(pair.shape[0])
    fill = jnp.full_like(pair, other)
    return jnp.where(low, pair, fill) if half == 0 else jnp.where(low, fill, pair)


def cols(ref, c):
    return ref[:, c * PAIR:(c + 1) * PAIR]


def block_of(refs):
    return functools.reduce(jnp.add, [ref[...] for ref in refs])


def weigh_head(q_pair, k_pairs, half):
    q_one = half_of(q_pair, half, 0)
    scores = [lax.dot_general(q_one, k, NT, preferred_element_type=jnp.float32) for k in k_pairs]
    top = functools.reduce(jnp.maximum, [jnp.max(s, axis=-1, keepdims=True) for s in scores])
    return top, [jnp.exp(s - top).astype(jnp.bfloat16) for s in scores]


def scaled(q_pair):
    return q_pair * jnp.asarray(HEAD_DIM ** -0.5, q_pair.dtype)


def add_values(weights, v_pairs, half):
    parts = [
        jnp.dot(w, half_of(v, half, 1), preferred_element_type=jnp.float32)
        for w, v in zip(weights, v_pairs)
    ]
    return functools.reduce(jnp.add, parts)


def numer_denom(first, second):
    low = low_lanes(first.shape[0])
    denom = pltpu.roll(jnp.where(low, second, first), HEAD_DIM, 1)
    return jnp.where(low, first, second), denom


def joined(states):
    top = functools.reduce(jnp.maximum, [t for t, _, _ in states])
    factors = [jnp.exp(t - top) for t, _, _ in states]
    numer = functools.reduce(jnp.add, [n * f for (_, n, _), f in zip(states, factors)])
    denom = functools.reduce(jnp.add, [d * f for (_, _, d), f in zip(states, factors)])
    return top, numer, denom


def kernel_call(body, outs, args, name):
    return pl.pallas_call(
        body,
        out_shape=[pltpu.VMEM(o.shape, o.dtype) for o in outs],
        in_specs=[SMEM if a.dtype == jnp.int32 else VMEM for a in args],
        out_specs=[VMEM] * len(outs),
        compiler_params=pltpu.CompilerParams(vmem_limit_bytes=VMEM_LIMIT),
        cost_estimate=COST,
        name=name,
    )(*args)


def whole(array):
    return [(array, 0, array.shape[1])]


def pairs_call(body, outs, operands, pairs, total, name):
    arrays, places = [], {}
    for c in pairs:
        for number, operand in enumerate(operands):
            share = sum(count for _, _, count in operand) // total
            at = c * share
            for array, first, count in operand:
                if 0 <= at < count:
                    if not any(array is other for other in arrays):
                        arrays.append(array)
                    index = [array is other for other in arrays].index(True)
                    places[c, number] = index, slice(first + at, first + at + share)
                at -= count

    def every_pair(*refs):
        for c in pairs:
            spots = [places[c, number] for number in range(len(operands))]
            ins = [refs[index].at[:, part] for index, part in spots]
            results = []
            for ref in refs[len(arrays):]:
                share = ref.shape[1] // len(pairs)
                at = (c - pairs.start) * share
                results.append(ref.at[:, at:at + share])
            body(*ins, *results)

    return kernel_call(every_pair, outs, arrays, name)


def attend(q, blocks, before, name):
    tokens, width = q.shape
    operands = [whole(q)] + [x for block in blocks for x in block]
    count = len(operands)
    operands += [whole(x) for x in before or []]

    def body(*refs):
        outs = refs[-3:]
        q_pair = scaled(refs[0][...])
        k_pairs = [r[...] for r in refs[1:count:2]]
        v_pairs = [r[...] for r in refs[2:count:2]]
        tops, sums = [], []
        for half in range(2):
            top, weights = weigh_head(q_pair, k_pairs, half)
            tops.append(top)
            sums.append(add_values(weights, v_pairs, half))
        state = (jnp.where(low_lanes(tokens), *tops), *numer_denom(*sums))
        if before is not None:
            state = joined([state, tuple(r[...] for r in refs[count:-3])])
        for out, value in zip(outs, state):
            out[...] = value

    outs = [jax.ShapeDtypeStruct((tokens, width), jnp.float32)] * 3
    return pairs_call(body, outs, operands, range(width // PAIR), width // PAIR, name)


def weigh(q, blocks, name):
    tokens, width = q.shape
    keys = blocks[0][0][0][0].shape[0]
    count = len(blocks)

    def body(q_ref, *refs):
        w_out, top_out = refs[-2:]
        q_pair = scaled(q_ref[...])
        rest = list(refs[:-2])
        k_pairs = [block_of([rest.pop(0) for _ in block]) for block in blocks]
        tops = []
        for half in range(2):
            top, weights = weigh_head(q_pair, k_pairs, half)
            tops.append(top)
            for i, w in enumerate(weights):
                at = (half * count + i) * keys
                w_out[:, at:at + keys] = w
        top_out[...] = jnp.where(low_lanes(tokens), *tops)

    outs = [
        jax.ShapeDtypeStruct((tokens, width // HEAD_DIM * count * keys), jnp.bfloat16),
        jax.ShapeDtypeStruct((tokens, width), jnp.float32),
    ]
    operands = [whole(q)] + [part for block in blocks for part in block]
    return pairs_call(body, outs, operands, range(width // PAIR), width // PAIR, name)


def gather(before, weighed, blocks, low_rank, pairs, name):
    weights, tops = weighed
    tokens, width = tops.shape
    count = len(blocks)
    keys = weights.shape[1] // (width // HEAD_DIM) // count
    operands = [whole(x) for x in (*before, weights, tops)]
    operands += [part for block in blocks for part in block]
    if low_rank is not None:
        operands.append(whole(low_rank))

    def body(*refs):
        rest = list(refs[5:len(operands)])
        v_pairs = [block_of([rest.pop(0) for _ in block]) for block in blocks]
        sums = []
        for half in range(2):
            ats = [(half * count + i) * keys for i in range(count)]
            sums.append(add_values([refs[3][:, at:at + keys] for at in ats], v_pairs, half))
        state = joined([tuple(r[...] for r in refs[:3]), (refs[4][...], *numer_denom(*sums))])
        if low_rank is not None:
            state = [(state[1] / state[2] + rest[0][...]).astype(jnp.bfloat16)]
        for out, value in zip(refs[len(operands):], state):
            out[...] = value

    if low_rank is not None:
        outs = [jax.ShapeDtypeStruct((tokens, len(pairs) * PAIR), jnp.bfloat16)]
        return pairs_call(body, outs, operands, pairs, width // PAIR, name)[0]
    outs = [jax.ShapeDtypeStruct((tokens, width), jnp.float32)] * 3
    return pairs_call(body, outs, operands, pairs, width // PAIR, name)


def finish(q, parts, before, low_rank, pairs, name):
    tokens, width = q.shape
    count = len(parts)
    operands = [whole(q)] + [k for k, _ in parts] + [v for _, v in parts]
    operands += [whole(x) for x in (*before, low_rank)]

    def body(*refs):
        q_pair = scaled(refs[0][...])
        k_pair, v_pair = block_of(refs[1:1 + count]), block_of(refs[1 + count:1 + 2 * count])
        tops, sums = [], []
        for half in range(2):
            top, weights = weigh_head(q_pair, [k_pair], half)
            tops.append(top)
            sums.append(add_values(weights, [v_pair], half))
        state = (jnp.where(low_lanes(tokens), *tops), *numer_denom(*sums))
        _, numer, denom = joined([state, tuple(r[...] for r in refs[1 + 2 * count:-2])])
        refs[-1][...] = (numer / denom + refs[-2][...]).astype(jnp.bfloat16)

    outs = [jax.ShapeDtypeStruct((tokens, len(pairs) * PAIR), jnp.bfloat16)]
    return pairs_call(body, outs, operands, pairs, width // PAIR, name)[0]


def twice(feat):
    return jnp.concatenate([feat, feat], axis=0)


def state_rows(pairs, features):
    return pairs * features + features


def key_state(k, v, feat, pairs):
    features = feat.shape[1]
    spread = PAIR // (2 * pairs)
    arrays = []
    for array, _, _ in k + v:
        if not any(array is other for other in arrays):
            arrays.append(array)

    def pair_of(refs, operand, c):
        at = c * PAIR
        for array, first, count in operand:
            if 0 <= at < count:
                index = [array is other for other in arrays].index(True)
                return refs[index][:, first + at:first + at + PAIR]
            at -= count

    count = len(arrays) + 1

    def body(*refs):
        out, done = refs[count], refs[-1]
        copies = []
        for c in range(pairs):
            part = pl.ds(c * PAIR, PAIR)
            copies.append([
                pltpu.make_async_copy(refs[i].at[:, part], refs[count + 1 + i].at[:, part], done.at[i, c])
                for i in range(count - 1)
            ])
        copies[0].insert(0, pltpu.make_async_copy(refs[count - 1], refs[2 * count], done.at[count - 1, 0]))
        for group in copies:
            for copy in group:
                copy.start()
        for copy in copies[0]:
            copy.wait()
        refs = refs[count + 1:-1]
        feat_ref = refs[-1]
        feat_t = twice(feat_ref[...].astype(jnp.float32)).T.astype(jnp.bfloat16)
        lane = lax.broadcasted_iota(jnp.int32, (features, PAIR), 1)
        norms = jnp.zeros((features, PAIR), jnp.float32)
        for c in range(pairs):
            for copy in copies[c] if c else []:
                copy.wait()
            k_pair, v_pair = pair_of(refs, k, c), pair_of(refs, v, c)
            k_float = k_pair.astype(jnp.float32)
            square = k_float * k_float
            square_hi = square.astype(jnp.bfloat16)
            square_lo = (square - square_hi.astype(jnp.float32)).astype(jnp.bfloat16)
            parts = []
            for half in range(2):
                proj = lax.dot_general(
                    half_of(feat_t, half, 0), k_pair, NT, preferred_element_type=jnp.float32
                )
                ones = half_of(jnp.ones((16, PAIR), jnp.bfloat16), half, 0)
                size = lax.dot_general(ones, square_hi, NT, preferred_element_type=jnp.float32)
                size += lax.dot_general(ones, square_lo, NT, preferred_element_type=jnp.float32)
                phi = jnp.exp(
                    proj * HEAD_DIM ** -0.25 - size[0:1, :] * (0.5 * HEAD_DIM ** -0.5)
                ).astype(jnp.bfloat16)
                parts.append(
                    jnp.dot(phi, half_of(v_pair, half, 1), preferred_element_type=jnp.float32)
                )
            out[c * features:(c + 1) * features, :] = jnp.where(
                low_lanes(features), parts[0], parts[1]
            ).astype(jnp.bfloat16)
            for half in range(2):
                at = (2 * c + half) * spread
                column = parts[half][:, (1 - half) * HEAD_DIM:(1 - half) * HEAD_DIM + 1]
                norms = jnp.where((lane >= at) & (lane < at + spread), column, norms)
        out[pairs * features:, :] = norms.astype(jnp.bfloat16)

    outs = jax.ShapeDtypeStruct((state_rows(pairs, features), PAIR), jnp.bfloat16)
    args = arrays + [feat]
    return pl.pallas_call(
        body,
        out_shape=pltpu.VMEM(outs.shape, outs.dtype),
        in_specs=[pl.BlockSpec(memory_space=pl.ANY)] * count,
        out_specs=VMEM,
        scratch_shapes=[pltpu.VMEM(x.shape, x.dtype) for x in args]
        + [pltpu.SemaphoreType.DMA((count, pairs))],
        compiler_params=pltpu.CompilerParams(vmem_limit_bytes=VMEM_LIMIT),
        cost_estimate=COST,
        name="key_state",
    )(*args)


def low_rank_rows(q, feat, state):
    tokens, width = q.shape
    pairs, features = width // PAIR, feat.shape[1]
    spread = PAIR // (2 * pairs)

    def body(q_ref, feat_ref, state_ref, out):
        feat_two = twice(feat_ref[...])
        norms = state_ref[pairs * features:, :]
        for c in range(pairs):
            q_pair = cols(q_ref, c)
            kv = state_ref[c * features:(c + 1) * features, :]
            low = low_lanes(features)
            parts = []
            for half in range(2):
                proj = jnp.dot(
                    half_of(q_pair, half, 0), feat_two, preferred_element_type=jnp.float32
                ) * HEAD_DIM ** -0.25
                phi = jnp.exp(proj - jnp.max(proj, axis=-1, keepdims=True)).astype(jnp.bfloat16)
                at = (2 * c + half) * spread
                column = jnp.broadcast_to(norms[:, at:at + 1], kv.shape)
                both = jnp.where(low, kv, column) if half == 0 else jnp.where(low, column, kv)
                parts.append(jnp.dot(phi, both, preferred_element_type=jnp.float32))
            numer, denom = numer_denom(*parts)
            out[:, c * PAIR:(c + 1) * PAIR] = numer / denom

    outs = jax.ShapeDtypeStruct((tokens, width), jnp.float32)
    return kernel_call(body, [outs], [q, feat, state], "low_rank")[0]


def project(acc, parts, name):
    tokens, width = parts[0][0].shape[0], parts[0][1].shape[1]
    arrays = []
    for array in [x for rows, w, _ in parts for x in (rows, w)] + ([] if acc is None else [acc]):
        if not any(array is other for other in arrays):
            arrays.append(array)

    def body(*refs):
        def ref_of(array):
            return refs[[array is other for other in arrays].index(True)]

        total = None if acc is None else ref_of(acc)[...]
        for rows, w, first in parts:
            w_rows = ref_of(w)[first:first + rows.shape[1], :]
            part = jnp.dot(ref_of(rows)[...], w_rows, preferred_element_type=jnp.float32)
            total = part if total is None else total + part
        refs[-1][...] = total.astype(refs[-1].dtype)

    if acc is None:
        outs = [jax.ShapeDtypeStruct((tokens, width), jnp.float32)]
        return kernel_call(body, outs, arrays, name)[0]
    return pl.pallas_call(
        body,
        out_shape=jax.ShapeDtypeStruct((tokens, width), jnp.bfloat16),
        in_specs=[VMEM] * len(arrays),
        out_specs=VMEM,
        compiler_params=pltpu.CompilerParams(vmem_limit_bytes=VMEM_LIMIT),
        cost_estimate=COST,
        name=name,
    )(*arrays)


def parted(array, place, bit, axis, name):
    shape = list(array.shape)
    shape[axis] //= 2
    half = shape[axis]

    def body(place_ref, ref, kept, sent):
        mine = (place_ref[0] >> bit) & 1
        for out, at in ((kept, mine), (sent, 1 - mine)):
            rows = pl.ds(pl.multiple_of(at * half, half), half)
            out[...] = ref[rows, :] if axis == 0 else ref[:, rows]

    outs = [jax.ShapeDtypeStruct(tuple(shape), array.dtype)] * 2
    return kernel_call(body, outs, [place, array], name)


def packed(k, v, name):
    tokens, width = k.shape

    def body(k_ref, v_ref, out, done):
        copies = [
            pltpu.make_async_copy(ref, out.at[:, pl.ds(at, width)], done.at[i])
            for i, (ref, at) in enumerate(((k_ref, 0), (v_ref, width)))
        ]
        for copy in copies:
            copy.start()
        for copy in copies:
            copy.wait()

    return pl.pallas_call(
        body,
        out_shape=pltpu.VMEM((tokens, 2 * width), k.dtype),
        in_specs=[pl.BlockSpec(memory_space=pl.ANY)] * 2,
        out_specs=VMEM,
        scratch_shapes=[pltpu.SemaphoreType.DMA((2,))],
        cost_estimate=COST,
        name=name,
    )(k, v)


def quarters(state, place, name):
    rows = state.shape[0] // 4

    def body(place_ref, ref, *outs):
        mine = place_ref[0] & 3
        for step, out in enumerate(outs):
            at = pl.multiple_of((mine ^ step) * rows, rows)
            out[...] = ref[pl.ds(at, rows), :]

    outs = [jax.ShapeDtypeStruct((rows, state.shape[1]), state.dtype)] * 4
    return kernel_call(body, outs, [place, state], name)


def added(arrays, name):
    def body(*refs):
        total = functools.reduce(jnp.add, [ref[...].astype(jnp.float32) for ref in refs[:-1]])
        refs[-1][...] = total.astype(refs[-1].dtype)

    outs = [jax.ShapeDtypeStruct(arrays[0].shape, arrays[0].dtype)]
    return kernel_call(body, outs, list(arrays), name)[0]


def whole_state(parts, place, name):
    rows = parts[0].shape[0]

    def body(place_ref, *refs):
        mine = place_ref[0] & 3
        for step, ref in enumerate(refs[:-1]):
            at = pl.multiple_of((mine ^ step) * rows, rows)
            refs[-1][pl.ds(at, rows), :] = ref[...]

    outs = [jax.ShapeDtypeStruct((4 * rows, parts[0].shape[1]), parts[0].dtype)]
    return kernel_call(body, outs, [place] + list(parts), name)[0]


def swapped(shard, axis, distance):
    return lax.ppermute(shard, axis, [(i, i ^ distance) for i in range(lax.axis_size(axis))])


def moved(shard, steps):
    span = lax.axis_size("seq") // 4
    return lax.ppermute(
        shard, "seq", [(a * span + r, b * span + r) for a, b in steps for r in range(span)]
    )


def every_distance(q, k, v, feat, w):
    index = lax.axis_index("seq").astype(jnp.int32).reshape(1)
    core = lax.axis_index("head").astype(jnp.int32).reshape(1)
    width = q.shape[1]

    first_steps = [(1, 3), (2, 0), (0, 1), (3, 2)]
    second_steps = [(1, 2), (2, 1)]
    edge_steps = [(1, 0), (2, 3)]
    after = lax.optimization_barrier
    pairs = width // PAIR
    split = pairs // 2 * PAIR

    k, index, core = after((k, index, core))
    k_1 = moved(k, first_steps)
    state = key_state(whole(k), whole(v), feat, pairs)
    kept, *sent = quarters(state, index, "state_quarters")
    got = [swapped(part, "seq", d) for part, d in zip(sent, (1, 2, 3))]
    got, k_next, v_next = after((got, k, v))
    v_1 = moved(v_next, first_steps)
    k_near = [swapped(k_next, "seq", d) for d in (1, 2)]
    state = added([kept] + got, "state_plane")
    state, k_1 = after((state, k_1))
    got = swapped(state, "seq", 4)
    sums = attend(q, [(whole(k), whole(v))], None, "attend_own")
    first = weigh(q, [[whole(k_1)]], "weigh_first")
    first, w, v_next = after((first, w, v))
    v_near = swapped(v_next, "seq", 1)
    w_own, w_sent = parted(w, core, 0, 1, "weights_parted")

    got, k_1, v_1, w_sent, sums, k_next, v_next = after((got, k_1, v_1, w_sent, sums, k, v))
    state = added([state, got], "state_line")
    got = swapped(state, "seq", 8)
    k_2 = moved(k_1, second_steps)
    k_3 = moved(k_next, edge_steps)
    v_last = swapped(v_next, "seq", 2)
    everyone = range(pairs)
    sums = gather(sums, first, [[whole(v_1)]], None, everyone, "gather_first")
    near = weigh(q, [[whole(far)] for far in k_near], "weigh_near")

    got, v_1 = after((got, v_1))
    v_2 = moved(v_1, second_steps)
    v_next, near, sums, v_near = after((v, near, sums, v_near))
    v_3 = moved(v_next, edge_steps)
    v_near = [v_near, v_last]
    v_near, got, sums, near, k_2, k_3 = after((v_near, got, sums, near, k_2, k_3))
    last = weigh(q, [[whole(k_2), whole(k_3)]], "weigh_last")
    state = added([state, got], "state_summed")
    got = [swapped(state, "seq", d) for d in (1, 2, 3)]
    sums = gather(sums, near, [[whole(far)] for far in v_near], None, everyone, "gather_near")
    got, sums, last, w_sent = after((got, sums, last, w_sent))
    w_far = swapped(w_sent, "head", 1)
    state = whole_state([state] + got, index, "state_whole")
    low = low_rank_rows(q, feat, state)

    v_last = [[whole(v_2), whole(v_3)]]
    rows_a = gather(sums, last, v_last, low, range(0, pairs // 2), "gather_a")
    far_a = swapped(rows_a, "head", 1)
    rows_b = gather(sums, last, v_last, low, range(pairs // 2, pairs), "gather_b")
    far_b = swapped(rows_b, "head", 1)
    acc = project(None, [(rows_a, w_own, 0), (far_a, w_far, 0), (rows_b, w_own, split)], "project_a")
    return project(acc, [(far_b, w_far, split)], "project_b")


def chosen_distances(q, k, v, distances, feat, w):
    state = key_state(whole(k), whole(v), feat, q.shape[1] // PAIR).astype(jnp.float32)
    state = lax.psum(state, "seq").astype(jnp.bfloat16)
    bits = lax.axis_size("seq").bit_length() - 1
    bit_ids = jnp.arange(bits, dtype=jnp.int32)
    powers = jnp.left_shift(jnp.ones((bits,), jnp.int32), bit_ids)

    def path(bit):
        return lambda pair: (swapped(pair[0], "seq", 1 << bit), swapped(pair[1], "seq", 1 << bit))

    paths = [path(bit) for bit in range(bits)]
    low = low_rank_rows(q, feat, state)
    sums = attend(q, [(whole(k), whole(v))], None, "attend_own")
    for partner in range(PARTNERS):
        picked = jnp.sum(jnp.where(distances[partner] == powers, bit_ids, 0))
        far = [whole(x) for x in lax.switch(picked, paths, (k, v))]
        if partner < PARTNERS - 1:
            sums = attend(q, [far], sums, "attend_far")
    rows = finish(q, [far], sums, low, range(q.shape[1] // PAIR), "finish")
    part = jnp.dot(rows, w, preferred_element_type=jnp.float32)
    return lax.psum_scatter(part.astype(jnp.bfloat16), "head", scatter_dimension=1, tiled=True)


def per_device(queries, keys, values, distances, feature_proj, out_proj):
    if lax.axis_size("seq") == 1 << PARTNERS and lax.axis_size("head") == 2:
        return every_distance(queries, keys, values, feature_proj, out_proj)
    return chosen_distances(queries, keys, values, distances, feature_proj, out_proj)


def solution(mesh):
    in_specs = (P("seq", "head"), P("seq", "head"), P("seq", "head"), P(), P(), P("head", None))
    return jax.shard_map(
        per_device, mesh=mesh, in_specs=in_specs, out_specs=P("seq", "head"), check_vma=False
    )
```
